256 devices in a mesh: row: 64 (over z, x, core), rep: 4 (over y).
Axes of the slice: x: 4, y: 4, z: 8, core: 2. Of those that a mesh axis runs over, the one named last changes fastest.
Arguments:
- features: bfloat16 [32768, 256], P(('row', 'rep')), may hold values from -6 to 6
- weight: bfloat16 [256, 256], replicated, may hold values from -0.375 to 0.375
- bias: float32 [256], replicated, may hold values from -3 to 3
- cotangent: bfloat16 [32768, 256], P(('row', 'rep')), may hold values from -6 to 6
- tile_values: bfloat16 [64, 4, 192, 128, 128], P('row', 'rep')
- tile_rows: int32 [64, 4, 192], P('row', 'rep'), may hold values from 0 to 3, as said below
- tile_cols: int32 [64, 4, 192], P('row', 'rep'), may hold values from 0 to 63, as said below
- tile_count: int32 [64, 4], P('row', 'rep'), may hold values from 1 to 192, as said below
Outputs:
- activation: bfloat16 [32768, 256], P(('row', 'rep'))
- grad_features: bfloat16 [32768, 256], P(('row', 'rep'))
- grad_weight: float32 [256, 256], replicated
- grad_bias: float32 [256], replicated
The draws below stay inside these ranges and needn't reach their ends.
Inputs may be any that keep to these rules, and one draw needn't show every extreme that they name: `tile_rows`: tile row of a slot, below 4; the (row, column) pairs of the 192 slots of one row block and column group are distinct. `tile_cols`: tile column of a slot within its column group. `tile_count`: slots at or past the count hold arbitrary values and are ignored; some row block and column group fills all 192 slots.
All inputs are finite; a program needn't handle non-finite values.
Results may differ from the reference program's by a relative error of at most 0.0075.
Values may be sent and summed in bfloat16 or wider, within the bound.
A program may use at most 128 MiB of HBM per device.

```python
import jax
import jax.numpy as jnp
from jax import lax

FEAT = 256
TILE = 128
R_DEV = 128
BLOCKS = 64
GROUPS = 4
NODES = 32768
TILES = 192


def tile_slots(key):
    count = BLOCKS * GROUPS
    places = GROUPS * R_DEV // TILE * (BLOCKS * R_DEV // TILE)
    keys = jax.random.split(jax.random.fold_in(key, 5), count)
    chosen = jax.vmap(lambda k: jax.random.permutation(k, places)[:TILES])(keys)
    return chosen.astype(jnp.int32).reshape(BLOCKS, GROUPS, TILES)


def draw_tile_rows(key, part):
    slots = tile_slots(key)
    return (slots // (BLOCKS * R_DEV // TILE)).astype(jnp.int32)


def draw_tile_cols(key, part):
    slots = tile_slots(key)
    return (slots % (BLOCKS * R_DEV // TILE)).astype(jnp.int32)


def draw_tile_count(key, part):
    key = jax.random.fold_in(key, 23)
    first, second, third = jax.random.split(key, 3)
    count = BLOCKS * GROUPS
    lowest = max(TILES // 8, 1)
    left = jax.random.randint(first, (count,), lowest, TILES + 1)
    right = jax.random.randint(second, (count,), lowest, TILES + 1)
    fewer = jnp.minimum(left, right)
    fullest = jax.random.randint(third, (), 0, count)
    fewer = jnp.where(jnp.arange(count, dtype=jnp.int32) == fullest, TILES, fewer)
    return fewer.astype(jnp.int32).reshape(BLOCKS, GROUPS)


def draw_tile_values(key, part):
    key = jax.random.fold_in(key, 24)
    first = jax.random.fold_in(key, 0)
    trows = GROUPS * R_DEV // TILE
    scale = 1.5 * (TILES * TILE / trows) ** (-0.5)
    shape = (BLOCKS, GROUPS, TILES, TILE, TILE)
    values = jax.random.normal(first, shape, jnp.float32) * scale
    return values.astype(jnp.bfloat16)


def block_levels(stream_key, dims, cuts, smallest, largest):
    def one(dim, shards_of):
        steps = jax.random.uniform(jax.random.fold_in(jax.random.fold_in(stream_key, 6), dim), (shards_of,), jnp.float32, smallest / len(cuts), largest / len(cuts))
        return jnp.repeat(jnp.exp(steps), dims[dim] // shards_of).reshape((-1,) + (1,) * (len(dims) - dim - 1))

    factor_of = one(*cuts[0])
    for cut in cuts[1:]:
        factor_of = factor_of * one(*cut)
    return factor_of


def scatter_about(stream_key, extent, spread, most, pieces=(), kind=jnp.bfloat16):
    level = block_levels(stream_key, extent, pieces, -0.22, 0.18) if pieces else 1.0
    entries = jax.random.normal(stream_key, extent, jnp.float32) * spread * level
    return jnp.minimum(jnp.maximum(entries, -most), most).astype(kind)


def setup_inputs(seed: int = 0) -> dict:
    arg_keys = jax.random.split(jax.random.key(seed), 9)
    return {
        "features": scatter_about(arg_keys[0], (NODES, FEAT), 1.0, 6.0, ((0, 256),)),
        "weight": scatter_about(arg_keys[1], (FEAT, FEAT), FEAT ** -0.5, 0.375),
        "bias": scatter_about(arg_keys[2], (FEAT,), 0.5, 3.0, (), jnp.float32),
        "cotangent": scatter_about(arg_keys[3], (NODES, FEAT), 1.0, 6.0, ((0, 256),)),
        "tile_values": draw_tile_values(jax.random.fold_in(arg_keys[8], 71), 0),
        "tile_rows": draw_tile_rows(jax.random.fold_in(arg_keys[8], 71), 0),
        "tile_cols": draw_tile_cols(jax.random.fold_in(arg_keys[8], 71), 0),
        "tile_count": draw_tile_count(jax.random.fold_in(arg_keys[8], 71), 0),
    }


def reference(features, weight, bias, cotangent, tile_values, tile_rows, tile_cols, tile_count):
    feat = features.shape[1]
    tile = TILE
    trows = GROUPS * R_DEV // tile
    tcols = BLOCKS * R_DEV // tile
    highest = lax.Precision.HIGHEST
    xw = jnp.dot(features, weight, preferred_element_type=jnp.float32).astype(jnp.bfloat16)
    group_tiles = jnp.transpose(xw.reshape(BLOCKS, GROUPS, R_DEV, feat), (1, 0, 2, 3)).reshape(GROUPS, tcols, tile, feat)
    live = (jnp.arange(TILES, dtype=jnp.int32)[None, None, :] < tile_count[:, :, None]).astype(jnp.float32)
    group_index = jnp.arange(GROUPS, dtype=jnp.int32)[:, None]

    def forward_block(items):
        values, rows, cols, alive = items
        taken = group_tiles[group_index, cols].astype(jnp.float32)
        prod = jnp.einsum('gkab,gkbf->gkaf', values.astype(jnp.float32), taken, precision=highest)
        onehot = (rows[:, :, None] == jnp.arange(trows, dtype=jnp.int32)[None, None, :]).astype(jnp.float32) * alive[:, :, None]
        part = jnp.einsum('gkr,gkaf->raf', onehot, prod, precision=highest)
        return part.reshape(GROUPS * R_DEV, feat)
    pre_blocks = lax.map(forward_block, (tile_values, tile_rows, tile_cols, live))
    pre = pre_blocks.reshape(NODES, feat) + bias[None, :]
    sig = jax.nn.sigmoid(pre)
    activation = (pre * sig).astype(jnp.bfloat16)
    dpre = (cotangent.astype(jnp.float32) * sig * (1.0 + pre * (1.0 - sig))).astype(jnp.bfloat16)
    dtiles_all = dpre.reshape(BLOCKS, trows, tile, feat)

    def backward_block(carry, items):
        values, rows, cols, alive, dtiles = items
        taken = dtiles[rows].astype(jnp.float32)
        prod = jnp.einsum('gkab,gkaf->gkbf', values.astype(jnp.float32), taken, precision=highest)
        prod = prod * alive[:, :, None, None]

        def one_group(p, c):
            return jax.ops.segment_sum(p, c, num_segments=tcols)
        contrib = jax.vmap(one_group)(prod, cols)
        return (carry + contrib, None)
    start = jnp.zeros((GROUPS, tcols, tile, feat), jnp.float32)
    back_groups, _ = lax.scan(backward_block, start, (tile_values, tile_rows, tile_cols, live, dtiles_all))
    back = jnp.transpose(back_groups.reshape(GROUPS, BLOCKS, R_DEV, feat), (1, 0, 2, 3)).reshape(NODES, feat)
    back_b = back.astype(jnp.bfloat16)
    grad_features = jnp.dot(back_b, weight.T, preferred_element_type=jnp.float32).astype(jnp.bfloat16)
    scale = 1.0 / jnp.sqrt(jnp.float32(NODES))
    grad_weight = jnp.dot(features.T, back_b, preferred_element_type=jnp.float32) * scale
    grad_bias = lax.optimization_barrier(jnp.sum(dpre.astype(jnp.float32), axis=0)) * scale
    return (activation, grad_features, grad_weight, grad_bias)
```

```python
import functools

import jax
import jax.numpy as jnp
from jax import lax
from jax.experimental import pallas as pl
from jax.experimental.pallas import tpu as pltpu
from jax.sharding import PartitionSpec as P

MESH = pl.DeviceIdType.MESH
F32 = jnp.float32
BF16 = jnp.bfloat16
NZ, NX, NY = 8, 4, 4
DZ = (0, 1, -1, 2, -2, 3, -3, 4)
DX = (0, 1, -1, 2)
GZ = ((0, 1), (1, 3), (3, 5), (5, 7), (7, 8))
GX = ((0, 1), (1, 3), (3, 4))
DIAGS = tuple(
    tuple((a, n - a) for a in range(4, -1, -1) if 0 <= n - a <= 2) for n in range(7)
)


def body(
    tile, slots, cut_rows, cut_feat, scale,
    features, weight, bias, cotangent, values_hbm, rows, cols, count,
    act_out, gf_out, gw_out, gb_out,
    values, inverse_v, inverse, gathered, acc, ysend, yrecv, dt,
    own32, own, sibsend, sibrecv, from_z, from_x,
    g1s, g1r, g2s, g2r, g3s, g3r, g4r, g5, g6, g7,
    send_sem, recv_sem, local_sem,
):
    r = lax.axis_index("row")
    y = lax.axis_index("rep")
    z = r // (2 * NX)
    x = (r // 2) % NX
    k = r % 2
    node_rows, feat = features.shape

    def at(zz, xx, kk, yy):
        return ((zz * NX + xx) * 2 + kk, yy)

    def z_off(d):
        return at((z + d + NZ) % NZ, x, k, y)

    def x_off(d):
        return at(z, (x + d + NX) % NX, k, y)

    def y_off(d):
        return at(z, x, k, (y + d + NY) % NY)

    sibling = at(z, x, 1 - k, y)
    z_far = at((z + 1 - 2 * k + NZ) % NZ, x, k, y)
    x_far = at(z, (x + 1 - 2 * k + NX) % NX, k, y)

    names = {}
    started = []

    def copy(name, src, dst, device):
        i = names.setdefault(name, len(names))
        return pltpu.make_async_remote_copy(
            src_ref=src, dst_ref=dst, send_sem=send_sem.at[i], recv_sem=recv_sem.at[i],
            device_id=device, device_id_type=MESH,
        )

    def send(name, src, dst, device):
        c = copy(name, src, dst, device)
        c.start()
        started.append(c)

    def arrived(name, dst):
        copy(name, dst, dst, sibling).wait_recv()

    tiles_in = pltpu.make_async_copy(
        values_hbm.at[0, 0], values.at[pl.ds(0, slots)], local_sem.at[0]
    )
    tiles_in.start()
    gathered[0, 0, 0] = features[...]
    barrier = pltpu.get_barrier_semaphore()
    peers = (
        [z_off(d) for d in range(1, NZ)]
        + [x_off(d) for d in range(1, NX)]
        + [y_off(d) for d in range(1, NY)]
        + [sibling]
    )
    for p in peers:
        pl.semaphore_signal(barrier, inc=1, device_id=p, device_id_type=MESH)
    pl.semaphore_wait(barrier, len(peers))

    part1 = pl.ds(0, cut_rows)
    part2 = pl.ds(cut_rows, node_rows - cut_rows)
    whole = pl.ds(0, node_rows)

    def span(pair):
        return pl.ds(pair[0], pair[1] - pair[0])

    def ag_z(a, b):
        part = whole if b == 0 else part2
        xs = span(GX[b])
        if a == 0:
            moves = ((0, 1, z_off(1)), (0, 2, z_off(-1)))
        elif a < 3:
            moves = ((2 * a - 1, 2 * a + 1, z_off(1)), (2 * a, 2 * a + 2, z_off(-1)))
        else:
            moves = ((5 + k, 7, z_far),)
        for n, (src, dst, dev) in enumerate(moves):
            send(("agz", a + 1, b, n), gathered.at[src, xs, 0, part], gathered.at[dst, xs, 0, part], dev)

    def ag_z_arrived(a, b):
        part = whole if b == 0 else part2
        for n, s in enumerate(range(*GZ[a])):
            arrived(("agz", a, b, n), gathered.at[s, span(GX[b]), 0, part])

    def ag_x(a, b):
        part = whole if a == 0 else part1
        zs = span(GZ[a])
        moves = ((0, 1, x_off(1)), (0, 2, x_off(-1))) if b == 0 else ((1 + k, 3, x_far),)
        for n, (src, dst, dev) in enumerate(moves):
            send(("agx", a, b + 1, n), gathered.at[zs, src, 0, part], gathered.at[zs, dst, 0, part], dev)

    def ag_x_arrived(a, b):
        part = whole if a == 0 else part1
        for n, s in enumerate(range(*GX[b])):
            arrived(("agx", a, b, n), gathered.at[span(GZ[a]), s, 0, part])

    def ag_pass(a, b):
        if a > 0:
            ag_z_arrived(a, b)
        if b > 0:
            ag_x_arrived(a, b)
        if a < 4:
            ag_z(a, b)
        if b < 2:
            ag_x(a, b)
        zs, xs = span(GZ[a]), span(GX[b])
        send(("ags", a, b), gathered.at[zs, xs, 0], gathered.at[zs, xs, 1], sibling)

    def offset_of(slot):
        half = (slot + 1) // 2
        return half * (2 * (slot % 2) - 1)

    def tile_of(tr, tc):
        p = tr * (NZ * NX * 2) + tc
        return values[inverse[p // 128, p % 128]]

    def tile_pair(tr, tc_own):
        other = tc_own + 1 - 2 * k
        return jnp.concatenate([tile_of(tr, tc_own), tile_of(tr, other)], axis=1)

    def col_of(zi, xi, sign):
        zz = (z + sign * offset_of(zi) + NZ) % NZ
        xx = (x + sign * offset_of(xi) + NX) % NX
        return (zz * NX + xx) * 2 + k

    def over_group(a, b, fn):
        (z0, z1), (x0, x1) = GZ[a], GX[b]
        n = (z1 - z0) * (x1 - x0)
        width = x1 - x0
        if n == 1:
            fn(z0, x0)
        else:
            def step(i, carry):
                fn(z0 + i // width, x0 + i % width)
                return carry
            lax.fori_loop(0, n, step, 0)

    def forward_chunk(zi, xi):
        tc = col_of(zi, xi, -1)
        lhs = jnp.concatenate([tile_pair((y + j) % NY, tc) for j in range(NY)], axis=0)
        rhs = gathered[zi, xi].reshape(2 * node_rows, feat)
        acc[...] += jnp.dot(lhs, rhs, preferred_element_type=F32)

    def ag_compute(a, b):
        zs, xs = span(GZ[a]), span(GX[b])
        arrived(("ags", a, b), gathered.at[zs, xs, 1])
        over_group(a, b, forward_chunk)

    ag_pass(0, 0)

    key = jnp.where(
        lax.broadcasted_iota(jnp.int32, (1, slots), 1) < count[...],
        rows[0] * (NZ * NX * 2) + cols[0], -1,
    )
    best = [jnp.full((1, 128), slots, jnp.int32) for _ in range(2)]
    for k0 in range(0, slots, 128):
        n = min(128, slots - k0)
        part = key[:, k0:k0 + n]
        if n < 128:
            part = jnp.concatenate([part, jnp.full((1, 128 - n), -1, jnp.int32)], axis=1)
        column = jnp.broadcast_to(part, (128, 128)).T
        slot = lax.broadcasted_iota(jnp.int32, (128, 128), 0) + k0
        for h in range(2):
            place = lax.broadcasted_iota(jnp.int32, (128, 128), 1) + h * 128
            hit = jnp.where(column == place, slot, slots)
            best[h] = jnp.minimum(best[h], jnp.min(hit, axis=0, keepdims=True))
    inverse_v[...] = jnp.concatenate(best + [jnp.full((6, 128), slots, jnp.int32)], axis=0)
    to_smem = pltpu.make_async_copy(inverse_v, inverse, local_sem.at[1])
    to_smem.start()
    values[slots] = jnp.zeros((tile, tile), BF16)
    acc[...] = jnp.zeros_like(acc)
    to_smem.wait()
    tiles_in.wait()

    for n in range(1, len(DIAGS)):
        for a, b in DIAGS[n]:
            ag_pass(a, b)
        for a, b in DIAGS[n - 1]:
            ag_compute(a, b)
    for a, b in DIAGS[-1]:
        ag_compute(a, b)

    for j in (2, 1, 3):
        ysend[j] = acc[pl.ds(j * node_rows, node_rows)].astype(BF16)
        send(("y", j), ysend.at[j], yrecv.at[j], y_off(j))
    agg = acc[pl.ds(0, node_rows)]
    for j in (1, 3, 2):
        arrived(("y", j), yrecv.at[j])
        agg = agg + yrecv[j].astype(F32)
    agg_hi = agg.astype(BF16)
    agg_lo = (agg - agg_hi.astype(F32)).astype(BF16)
    pre = (
        jnp.dot(agg_hi, weight[...], preferred_element_type=F32)
        + jnp.dot(agg_lo, weight[...], preferred_element_type=F32)
        + bias[...]
    )
    sig = jax.nn.sigmoid(pre)
    dpre = (cotangent[...].astype(F32) * sig * (1.0 + pre * (1.0 - sig))).astype(BF16)
    dt[0] = dpre.astype(F32).T.astype(BF16)
    for j in (2, 1, 3):
        send(("d", j), dt.at[0], dt.at[j], y_off(j))
    act_out[...] = (pre * sig).astype(BF16)

    half = feat // 2
    aggt_hi = agg_hi.astype(F32).T.astype(BF16)
    aggt_lo = agg_lo.astype(F32).T.astype(BF16)
    bias_row = jnp.sum(dpre.astype(F32), axis=0, keepdims=True)
    bias_rows = jnp.concatenate([bias_row, jnp.zeros((7, feat), F32)], axis=0)
    gw = jnp.dot(aggt_hi, dpre, preferred_element_type=F32) + jnp.dot(
        aggt_lo, dpre, preferred_element_type=F32
    )
    for h in range(2):
        g1s[h, pl.ds(0, half)] = gw[h * half:(h + 1) * half]
        g1s[h, pl.ds(half, 8)] = bias_rows
    send("g1", g1s.at[1 - k], g1r, sibling)

    yrows, xrows = half // NY, half // NY // NX

    def g_step(n):
        if n == 2:
            arrived("g1", g1r)
            total = g1s[k] + g1r[...]
            for c in range(NY):
                g2s[c, pl.ds(0, yrows)] = total[c * yrows:(c + 1) * yrows]
                g2s[c, pl.ds(yrows, 8)] = total[half:half + 8]
            for j in (2, 1, 3):
                send(("g2", j), g2s.at[(y + j) % NY], g2r.at[y], y_off(j))
            g2r[y] = g2s[y]
        elif n == 3:
            for j in (1, 3, 2):
                arrived(("g2", j), g2r.at[(y - j + NY) % NY])
            total = g2r[0] + g2r[1] + g2r[2] + g2r[3]
            for c in range(NX):
                g3s[c, pl.ds(0, xrows)] = total[c * xrows:(c + 1) * xrows]
                g3s[c, pl.ds(xrows, 8)] = total[yrows:yrows + 8]
            for j in (2, 1, 3):
                send(("g3", j), g3s.at[(x + j) % NX], g3r.at[x], x_off(j))
            g3r[x] = g3s[x]
        elif n == 4:
            for j in (1, 3, 2):
                arrived(("g3", j), g3r.at[(x - j + NX) % NX])
            g4r[z] = g3r[0] + g3r[1] + g3r[2] + g3r[3]
            for j in (4, 3, 5, 2, 6, 1, 7):
                send(("g4", j), g4r.at[z], g4r.at[z], z_off(j))
        elif n == 5:
            for j in (1, 7, 2, 6, 3, 5, 4):
                arrived(("g4", j), g4r.at[(z - j + NZ) % NZ])
            total = g4r[0]
            for j in range(1, NZ):
                total = total + g4r[j]
            total = total * scale
            gb_out[...] = total[xrows:xrows + 1]
            g5[x] = total[0:xrows]
            for j in (2, 1, 3):
                send(("g5", j), g5.at[x], g5.at[x], x_off(j))
        elif n == 6:
            for j in (1, 3, 2):
                arrived(("g5", j), g5.at[(x - j + NX) % NX])
            g6[y] = g5[...].reshape(yrows, feat)
            for j in (2, 1, 3):
                send(("g6", j), g6.at[y], g6.at[y], y_off(j))
        elif n == 7:
            for j in (1, 3, 2):
                arrived(("g6", j), g6.at[(y - j + NY) % NY])
            g7[k] = g6[...].reshape(half, feat)
            send("g7", g7.at[k], g7.at[k], sibling)
        elif n == 8:
            arrived("g7", g7.at[1 - k])
            gw_out[...] = g7[...].reshape(feat, feat)

    for j in (1, 3, 2):
        arrived(("d", j), dt.at[j])

    def backward_chunk(zi, xi):
        tc = col_of(zi, xi, 1)
        lhs = jnp.concatenate([dt[j] for j in range(NY)], axis=1)
        rhs = jnp.concatenate([tile_pair((y - j + NY) % NY, tc) for j in range(NY)], axis=0)
        both = jnp.dot(lhs, rhs, preferred_element_type=F32)
        own32[zi, xi] = both[:, :tile]
        sibsend[zi, xi] = both[:, tile:].astype(BF16)

    def rs_compute(a, b):
        over_group(a, b, backward_chunk)
        zs, xs = span(GZ[a]), span(GX[b])
        send(("rss", a, b), sibsend.at[zs, xs], sibrecv.at[zs, xs], sibling)

    fpart1, fpart2 = (0, cut_feat), (cut_feat, feat)
    fwhole = (0, feat)

    def rs_z(a, b):
        f = span(fwhole if b == 0 else fpart2)
        xs = span(GX[b])
        s = GZ[a][0]
        moves = ((s, z_far),) if a == 4 else ((s, z_off(1)), (s + 1, z_off(-1)))
        for n, (src, dev) in enumerate(moves):
            send(("rsz", a, b, n), own.at[src, xs, f], from_z.at[src, xs, f], dev)

    def rs_z_arrived(a, b):
        f = span(fwhole if b == 0 else fpart2)
        for n, s in enumerate(range(*GZ[a])):
            arrived(("rsz", a, b, n), from_z.at[s, span(GX[b]), f])

    def rs_x(a, b):
        f = span(fwhole if a == 0 else fpart1)
        zs = span(GZ[a])
        s = GX[b][0]
        moves = ((s, x_far),) if b == 2 else ((s, x_off(1)), (s + 1, x_off(-1)))
        for n, (src, dev) in enumerate(moves):
            send(("rsx", a, b, n), own.at[zs, src, f], from_x.at[zs, src, f], dev)

    def rs_x_arrived(a, b):
        f = span(fwhole if a == 0 else fpart1)
        for n, s in enumerate(range(*GX[b])):
            arrived(("rsx", a, b, n), from_x.at[span(GZ[a]), s, f])

    def rs_sum(a, b, zi, xi, part):
        f = span(part)
        total = own32[zi, xi, f] + sibrecv[zi, xi, f].astype(F32)
        if b == 0 or part == fpart2:
            if a == 3:
                total = total + jnp.where(zi == 5 + k, from_z[7, xi, f].astype(F32), 0.0)
            elif a in (1, 2):
                total = total + from_z[zi + 2, xi, f].astype(F32)
            elif a == 0:
                total = total + from_z[1, xi, f].astype(F32) + from_z[2, xi, f].astype(F32)
        if a == 0 or part == fpart1:
            if b == 1:
                total = total + jnp.where(xi == 1 + k, from_x[zi, 3, f].astype(F32), 0.0)
            elif b == 0:
                total = total + from_x[zi, 1, f].astype(F32) + from_x[zi, 2, f].astype(F32)
        return total

    def rs_pass(a, b):
        zs, xs = span(GZ[a]), span(GX[b])
        arrived(("rss", a, b), sibrecv.at[zs, xs])
        if a < 4:
            rs_z_arrived(a + 1, b)
        if b < 2:
            rs_x_arrived(a, b + 1)
        if (a, b) == (0, 0):
            return

        def one(zi, xi):
            for part in (fpart1, fpart2):
                own[zi, xi, span(part)] = rs_sum(a, b, zi, xi, part).astype(BF16)

        over_group(a, b, one)
        if a > 0:
            rs_z(a, b)
        if b > 0:
            rs_x(a, b)

    order = DIAGS[::-1]
    for n in range(len(order) + 1):
        if n < len(order):
            for a, b in order[n]:
                rs_compute(a, b)
        if n >= 1:
            for a, b in order[n - 1]:
                rs_pass(a, b)
            g_step(n + 1)

    back_t = jnp.concatenate([rs_sum(0, 0, 0, 0, p) for p in (fpart1, fpart2)], axis=0)
    gf_out[...] = lax.dot_general(
        back_t.T.astype(BF16), weight[...], (((1,), (1,)), ((), ())), preferred_element_type=F32
    ).astype(BF16)
    for c in started:
        c.wait_send()


COPIES = 160


def on_device(features, weight, bias, cotangent, tile_values, tile_rows, tile_cols, tile_count):
    node_rows, feat = features.shape
    slots, tile = tile_values.shape[2], tile_values.shape[-1]
    half = feat // 2
    yrows, xrows = half // NY, half // NY // NX
    blocks = NZ * NX * 2
    scale = float((node_rows * blocks * NY) ** -0.5)
    vmem = pl.BlockSpec(memory_space=pltpu.VMEM)
    act, gf, gw, gb = pl.pallas_call(
        functools.partial(body, tile, slots, 80, 160, scale),
        out_shape=(
            jax.ShapeDtypeStruct((node_rows, feat), BF16),
            jax.ShapeDtypeStruct((node_rows, feat), BF16),
            jax.ShapeDtypeStruct((feat, feat), F32),
            jax.ShapeDtypeStruct((1, feat), F32),
        ),
        in_specs=[vmem] * 4 + [pl.BlockSpec(memory_space=pl.ANY)] + [vmem] * 3,
        out_specs=(vmem,) * 4,
        scratch_shapes=[
            pltpu.VMEM((slots + 1, tile, tile), BF16),
            pltpu.VMEM((8, 128), jnp.int32),
            pltpu.SMEM((8, 128), jnp.int32),
            pltpu.VMEM((NZ, NX, 2, node_rows, feat), BF16),
            pltpu.VMEM((NY * node_rows, feat), F32),
            pltpu.VMEM((NY, node_rows, feat), BF16),
            pltpu.VMEM((NY, node_rows, feat), BF16),
            pltpu.VMEM((NY, feat, node_rows), BF16),
            pltpu.VMEM((NZ, NX, feat, tile), F32),
            pltpu.VMEM((NZ, NX, feat, tile), BF16),
            pltpu.VMEM((NZ, NX, feat, tile), BF16),
            pltpu.VMEM((NZ, NX, feat, tile), BF16),
            pltpu.VMEM((NZ, NX, feat, tile), BF16),
            pltpu.VMEM((NZ, NX, feat, tile), BF16),
            pltpu.VMEM((2, half + 8, feat), F32),
            pltpu.VMEM((half + 8, feat), F32),
            pltpu.VMEM((NY, yrows + 8, feat), F32),
            pltpu.VMEM((NY, yrows + 8, feat), F32),
            pltpu.VMEM((NX, xrows + 8, feat), F32),
            pltpu.VMEM((NX, xrows + 8, feat), F32),
            pltpu.VMEM((NZ, xrows + 8, feat), F32),
            pltpu.VMEM((NX, xrows, feat), F32),
            pltpu.VMEM((NY, yrows, feat), F32),
            pltpu.VMEM((2, half, feat), F32),
            pltpu.SemaphoreType.DMA((COPIES,)),
            pltpu.SemaphoreType.DMA((COPIES,)),
            pltpu.SemaphoreType.DMA((2,)),
        ],
        compiler_params=pltpu.CompilerParams(
            collective_id=0, has_side_effects=True, vmem_limit_bytes=48 * 1024 * 1024
        ),
        cost_estimate=pl.CostEstimate(
            flops=4 * NY * node_rows * blocks * node_rows * feat,
            bytes_accessed=slots * tile * tile * 2,
            transcendentals=node_rows * feat,
        ),
    )(features, weight, bias.reshape(1, feat), cotangent, tile_values, tile_rows, tile_cols, tile_count)
    return act, gf, gw, gb.reshape(feat)


def solution(mesh):
    in_specs = (
        P(("row", "rep"), None),
        P(),
        P(),
        P(("row", "rep"), None),
        P("row", "rep", None, None, None),
        P("row", "rep", None),
        P("row", "rep", None),
        P("row", "rep"),
    )
    out_specs = (P(("row", "rep"), None), P(("row", "rep"), None), P(), P())
    return jax.shard_map(
        on_device, mesh=mesh, in_specs=in_specs, out_specs=out_specs, check_vma=False
    )
```

```python
import functools

import jax
import jax.numpy as jnp
from jax import lax
from jax.experimental import pallas as pl
from jax.experimental.pallas import tpu as pltpu
from jax.sharding import PartitionSpec as P

MESH = pl.DeviceIdType.MESH
F32 = jnp.float32
BF16 = jnp.bfloat16
NZ, NX, NY = 8, 4, 4
Z_COLUMN = ({0: ((3, 2), (4, -2), (1, 1), (2, -1)), 3: ((5, 1),), 4: ((6, -1),)}, (3, 4), 7, 2)
X_ROW = ({0: ((3, 2), (1, 1), (2, -1))}, (), 0, 0)
X_FIRST = ({0: ((1, 1), (2, -1))}, (1, 2), 3, 1)
Z_SECOND = ({0: ((3, 2), (4, -2), (1, 1), (2, -1)), 3: ((5, 1),), 4: ((6, -1),)}, (3, 4), 7, 2)
Z_REACH, X_REACH = ((1, 2), (1, 2))
PARTS = ((1, 0, 96), (2, 96, 128))
AG_ORDER = (
    (0,0,0,0), (0,0,0,1), (1,0,0), (0,0,3,0), (0,3,0,0), (0,4,0,0), (0,0,1,0), (0,0,2,0), (0,1,0,0), (0,0,3,1),
    (0,2,0,0), (1,0,3), (0,0,2,1), (0,0,1,1), (1,0,2), (1,0,1), (0,3,0,1), (0,4,0,1), (1,3,0), (1,4,0), (0,1,0,1),
    (0,2,0,1), (1,1,0), (1,2,0), (0,3,1,0), (0,3,2,0), (2,(0,0),(0,3),(0,2),(0,1)), (0,5,0,0), (0,4,1,0), (0,4,2,0),
    (2,(3,0),(4,0),(1,0),(2,0)), (0,7,0,0), (0,1,1,0), (0,1,2,0), (0,3,3,1), (0,6,0,0), (0,1,3,1), (0,2,1,0),
    (0,2,2,0), (0,3,3,0), (1,3,3), (0,4,3,1), (0,3,2,1), (0,2,3,1), (1,3,2), (0,1,2,1), (1,1,2), (0,5,1,0), (0,5,2,0),
    (0,4,2,1), (1,4,2), (0,4,3,0), (1,4,3), (0,3,1,1), (0,2,2,1), (1,3,1), (1,2,2), (0,1,1,1), (1,1,1), (0,5,0,1),
    (1,5,0), (0,7,1,0), (0,7,2,0), (2,(3,3),(3,2),(1,2),(4,2)), (0,4,1,1), (1,4,1), (0,1,3,0), (0,2,1,1), (1,1,3),
    (1,2,1), (2,(4,3),(3,1),(2,2),(1,1)), (0,7,0,1), (1,7,0), (0,6,1,0), (0,6,2,0), (0,5,3,1), (0,6,0,1), (1,6,0),
    (0,2,3,0), (1,2,3), (0,7,3,1), (2,(5,0),(4,1),(1,3),(2,1)), (0,5,3,0), (1,5,3), (0,5,2,1), (0,6,3,1), (1,5,2),
    (0,7,3,0), (1,7,3), (0,7,2,1), (1,7,2), (2,(7,0),(6,0),(2,3),(5,3)), (0,6,3,0), (0,5,1,1), (0,6,2,1), (1,6,3),
    (1,5,1), (1,6,2), (0,7,1,1), (1,7,1), (0,6,1,1), (1,6,1), (2,(5,2),(7,3),(7,2),(6,3)), (2,(5,1),(6,2)),
    (2,(7,1),(6,1)),
)
RS_ORDER = (
    (2,(7,3),(5,3),(6,3),(7,1)), (2,(7,2),(5,1),(6,1),(6,2)), (2,(5,2),(4,3),(3,3),(1,3)), (0,7,3,0), (0,7,3,1),
    (0,5,3,0), (0,5,3,1), (0,6,3,0), (0,6,3,1), (2,(2,3),(7,0),(5,0),(6,0)), (0,7,1,1), (0,7,2,1), (0,5,1,1),
    (2,(3,1),(4,1),(4,2),(3,2)), (0,6,1,1), (0,6,2,1), (0,5,2,1), (2,(2,1),(1,1),(2,2),(1,2)), (0,4,3,0), (0,3,3,0),
    (0,1,3,0), (0,7,1,0), (0,7,2,0), (0,2,3,0), (0,7,0,1), (0,1,3,1), (0,5,1,0), (0,5,2,0), (0,3,3,1), (0,4,3,1),
    (0,2,3,1), (0,6,1,0), (0,6,2,0), (0,5,0,1), (0,6,0,1), (2,(4,0),(3,0),(0,3),(1,0)), (0,2,1,1), (0,4,1,0),
    (0,4,2,0), (0,1,1,1), (2,(2,0),(0,1),(0,2),(0,0)), (0,2,2,1), (0,3,1,0), (0,3,2,0), (0,1,2,1), (0,3,1,1),
    (0,4,1,1), (0,1,1,0), (0,4,2,1), (0,3,2,1), (0,1,2,0), (0,0,3,0), (0,1,0,1), (0,2,0,1), (0,7,0,0), (0,0,1,0),
    (0,2,1,0), (0,2,2,0), (0,0,2,0), (0,0,3,1), (0,5,0,0), (0,4,0,1), (0,3,0,1), (0,6,0,0), (0,0,1,1), (0,0,2,1),
    (0,1,0,0), (0,3,0,0), (0,4,0,0), (0,2,0,0), (0,0,0,1), (0,0,0,0),
)
G_AT = (34, 64, 69, 71)


def moves(kind, zi, xi):
    if kind == 1:
        if xi == 0:
            yield "z", zi, Z_COLUMN
        yield "x", xi, (X_FIRST if zi else X_ROW)
    else:
        if zi == 0:
            yield "x", xi, X_ROW
        yield "z", zi, (Z_SECOND if xi else Z_COLUMN)


def children(kind, zi, xi):
    found = []
    for axis, at, (steps, pair, last, hops) in moves(kind, zi, xi):
        for to, h in steps.get(at, ()):
            found.append((axis, (to, xi) if axis == "z" else (zi, to), h, None))
        if at in pair:
            found.append((axis, (last, xi) if axis == "z" else (zi, last), hops, pair.index(at)))
    return found


def body(
    tile, slots, scale,
    features_hbm, weight_hbm, bias_hbm, cotangent_hbm, values_hbm, rows_hbm, cols_hbm, count_hbm,
    act_out, gf_out, gw_out, gb_out,
    features, weight, bias, cotangent, rows, cols, count,
    values, inverse_v, inverse, gathered, acc, ysend, yrecv, dt,
    own32, own, sibsend, sibrecv, landed, back_t,
    g1s, g1r, g2s, g2r, g4r, g5, g7,
    send_sem, recv_sem, local_sem,
):
    r = lax.axis_index("row")
    y = lax.axis_index("rep")
    z = r // (2 * NX)
    x = (r // 2) % NX
    k = r % 2
    node_rows, feat = features_hbm.shape
    half = feat // 2

    def at(zz, xx, kk, yy):
        return ((zz * NX + xx) * 2 + kk, yy)

    def z_off(d):
        return at((z + d + NZ) % NZ, x, k, y)

    def x_off(d):
        return at(z, (x + d + NX) % NX, k, y)

    def y_off(d):
        return at(z, x, k, (y + d + NY) % NY)

    def toward(axis, hops, pair):
        d = hops if pair is None else hops * (1 - 2 * k)
        return z_off(d) if axis == "z" else x_off(d)

    sibling = at(z, x, 1 - k, y)
    names = {}
    groups = {}

    def copy(name, group, src, dst, device):
        i = names.setdefault(name, len(names))
        j = groups.setdefault(group, len(groups))
        return pltpu.make_async_remote_copy(
            src_ref=src, dst_ref=dst, send_sem=send_sem.at[j], recv_sem=recv_sem.at[i],
            device_id=device, device_id_type=MESH,
        )

    def send(name, group, src, dst, device):
        copy(name, group, src, dst, device).start()

    def arrived(name, dst):
        copy(name, "ag", dst, dst, sibling).wait_recv()

    def sent(group, src):
        copy("y", group, src, src, sibling).wait_send()

    loads = [
        pltpu.make_async_copy(src, dst, local_sem.at[n])
        for n, (src, dst) in enumerate((
            (features_hbm, features), (rows_hbm, rows), (cols_hbm, cols), (count_hbm, count),
            (weight_hbm, weight), (bias_hbm, bias), (cotangent_hbm, cotangent),
            (values_hbm.at[0, 0], values.at[pl.ds(0, slots)]),
        ))
    ]
    for load in loads:
        load.start()
    barrier = pltpu.get_barrier_semaphore()
    peers = (
        [z_off(s * d) for d in Z_REACH for s in (1, -1)]
        + [x_off(s * d) for d in X_REACH for s in (1, -1)]
        + [y_off(d) for d in range(1, NY)]
        + [sibling]
    )
    for p in peers:
        pl.semaphore_signal(barrier, inc=1, device_id=p, device_id_type=MESH)
    loads[0].wait()
    pl.semaphore_wait(barrier, len(peers))

    seen = set()

    def ag_piece(zi, xi, p):
        kind, r0, r1 = PARTS[p]
        part = pl.ds(r0, r1 - r0)
        if (zi, xi) == (0, 0):
            source = features.at[part]
        else:
            source = gathered.at[zi, xi, 0, part]
            arrived(("ag", zi, xi, p), source)
        for axis, (zd, xd), hops, pair in children(kind, zi, xi):
            origin = source
            if pair is not None:
                if (zd, xd, p) not in seen:
                    seen.add((zd, xd, p))
                    continue
                if axis == "z":
                    origin = gathered.at[zi - pair + k, xi, 0, part]
                else:
                    origin = gathered.at[zi, xi - pair + k, 0, part]
            send(("ag", zd, xd, p), "ag", origin, gathered.at[zd, xd, 0, part], toward(axis, hops, pair))

    batch_of = {c: n for n, (what, *where) in enumerate(AG_ORDER) if what == 2 for c in where}

    def ag_share(zi, xi):
        source = features if (zi, xi) == (0, 0) else gathered.at[zi, xi, 0]
        send(("share", batch_of[zi, xi]), "ag", source, gathered.at[zi, xi, 1], sibling)

    def offset_of(slot):
        return (slot + 1) // 2 * (2 * (slot % 2) - 1)

    def tile_of(tr, tc):
        p = tr * (NZ * NX * 2) + tc
        return values[inverse[p // 128, p % 128]]

    def tile_pair(tr, tc_own):
        return jnp.concatenate([tile_of(tr, tc_own), tile_of(tr, tc_own + 1 - 2 * k)], axis=1)

    def col_of(zi, xi, sign):
        zz = (z + sign * offset_of(zi) + NZ) % NZ
        xx = (x + sign * offset_of(xi) + NX) % NX
        return (zz * NX + xx) * 2 + k

    def forward(chunks):
        arrived(("share", batch_of[chunks[0]]), gathered.at[pl.ds(0, len(chunks)), 0, 1])
        lhs = jnp.concatenate([
            jnp.concatenate([tile_pair((y + j) % NY, col_of(zi, xi, -1)) for zi, xi in chunks], axis=1)
            for j in range(NY)
        ], axis=0)
        rhs = jnp.concatenate([gathered[zi, xi].reshape(2 * node_rows, feat) for zi, xi in chunks], axis=0)
        term = jnp.dot(lhs, rhs, preferred_element_type=F32)
        if (0, 0) in chunks:
            acc[...] = term
        else:
            acc[...] += term

    todo = list(AG_ORDER)
    while todo[0][:3] == (0, 0, 0):
        ag_piece(*todo.pop(0)[1:])
    gathered[0, 0, 0] = features[...]

    for load in loads[1:4]:
        load.wait()
    key = jnp.where(
        lax.broadcasted_iota(jnp.int32, (1, slots), 1) < count[...],
        rows[0] * (NZ * NX * 2) + cols[0], -1,
    )
    best = [jnp.full((1, 128), slots, jnp.int32) for _ in range(2)]
    for k0 in range(0, slots, 128):
        n = min(128, slots - k0)
        part = key[:, k0:k0 + n]
        if n < 128:
            part = jnp.concatenate([part, jnp.full((1, 128 - n), -1, jnp.int32)], axis=1)
        column = jnp.broadcast_to(part, (128, 128)).T
        slot = lax.broadcasted_iota(jnp.int32, (128, 128), 0) + k0
        for h in range(2):
            place = lax.broadcasted_iota(jnp.int32, (128, 128), 1) + h * 128
            hit = jnp.where(column == place, slot, slots)
            best[h] = jnp.minimum(best[h], jnp.min(hit, axis=0, keepdims=True))
    inverse_v[...] = jnp.concatenate(best + [jnp.full((6, 128), slots, jnp.int32)], axis=0)
    to_smem = pltpu.make_async_copy(inverse_v, inverse, local_sem.at[len(loads)])
    to_smem.start()
    values[slots] = jnp.zeros((tile, tile), BF16)

    ready = False
    for what, *where in todo:
        if what == 0:
            ag_piece(*where)
        elif what == 1:
            ag_share(*where)
        else:
            if not ready:
                to_smem.wait()
                for load in loads[4:]:
                    load.wait()
                ready = True
            forward(where)

    for j in (2, 1, 3):
        ysend[j] = acc[pl.ds(j * node_rows, node_rows)].astype(BF16)
        send("y", "yd", ysend.at[j], yrecv.at[j], y_off(j))
    agg = acc[pl.ds(0, node_rows)]
    arrived("y", yrecv.at[pl.ds(1, 3)])
    for j in (1, 3, 2):
        agg = agg + yrecv[j].astype(F32)
    agg_hi = agg.astype(BF16)
    agg_lo = (agg - agg_hi.astype(F32)).astype(BF16)
    halves = []
    for h in range(2):
        f = pl.ds(h * half, half)
        pre = (
            jnp.dot(agg_hi, weight[:, f], preferred_element_type=F32)
            + jnp.dot(agg_lo, weight[:, f], preferred_element_type=F32)
            + bias[:, f]
        )
        sig = jax.nn.sigmoid(pre)
        dpre = (cotangent[:, f].astype(F32) * sig * (1.0 + pre * (1.0 - sig))).astype(BF16)
        dt[0, f] = dpre.astype(F32).T.astype(BF16)
        for j in (2, 1, 3):
            send(("d", h), "yd", dt.at[0, f], dt.at[j, f], y_off(j))
        act_out[:, f] = (pre * sig).astype(BF16)
        halves.append(dpre)
    dpre = jnp.concatenate(halves, axis=1)

    aggt_hi = agg_hi.astype(F32).T.astype(BF16)
    aggt_lo = agg_lo.astype(F32).T.astype(BF16)
    bias_row = jnp.sum(dpre.astype(F32), axis=0, keepdims=True)
    bias_rows = jnp.concatenate([bias_row, jnp.zeros((7, feat), F32)], axis=0)
    gw = jnp.dot(aggt_hi, dpre, preferred_element_type=F32) + jnp.dot(
        aggt_lo, dpre, preferred_element_type=F32
    )
    for h in range(2):
        g1s[h, pl.ds(0, half)] = gw[h * half:(h + 1) * half]
        g1s[h, pl.ds(half, 8)] = bias_rows
    send("g1", "g1", g1s.at[1 - k], g1r, sibling)

    q = y * NX + x
    square = [(dy, dx) for dy in (2, 1, 3, 0) for dx in (2, 1, 3, 0) if (dy, dx) != (0, 0)]

    def in_square(dy, dx):
        yy, xx = (y + dy) % NY, (x + dx) % NX
        return yy * NX + xx, at(z, xx, k, yy)

    def g_step(n):
        if n == 0:
            arrived("g1", g1r)
            total = g1s[k] + g1r[...]
            for c in range(NY * NX):
                g2s[c, pl.ds(0, 8)] = total[c * 8:(c + 1) * 8]
                g2s[c, pl.ds(8, 8)] = total[half:half + 8]
            for dy, dx in square:
                c, device = in_square(dy, dx)
                send("g2", "g2", g2s.at[c], g2r.at[q], device)
            g2r[q] = g2s[q]
        elif n == 1:
            arrived("g2", g2r.at[pl.ds(0, NY * NX - 1)])
            total = g2r[0]
            for c in range(1, NY * NX):
                total = total + g2r[c]
            g4r[z] = total
            for j in (4, 3, 5, 2, 6, 1, 7):
                send("g4", "g4", g4r.at[z], g4r.at[z], z_off(j))
        elif n == 2:
            arrived("g4", g4r.at[pl.ds(0, NZ - 1)])
            total = g4r[0]
            for j in range(1, NZ):
                total = total + g4r[j]
            total = total * scale
            gb_out[...] = total[8:9]
            g5[q] = total[0:8]
            for dy, dx in square:
                send("g5", "g5", g5.at[q], g5.at[q], in_square(dy, dx)[1])
        elif n == 3:
            arrived("g5", g5.at[pl.ds(0, NY * NX - 1)])
            g7[k] = g5[...].reshape(half, feat)
            send("g7", "g7", g7.at[k], g7.at[k], sibling)
        elif n == 4:
            arrived("g7", g7.at[1 - k])
            gw_out[...] = g7[...].reshape(feat, feat)

    g_step(0)
    sent("ag", values.at[pl.ds(0, 2 * (2 * NZ * NX - 1))])

    for h in range(2):
        arrived(("d", h), dt.at[pl.ds(1, NY - 1), pl.ds(h * half, half)])

    back_batch = {c: n for n, (what, *where) in enumerate(RS_ORDER) if what == 2 for c in where}
    back_size = {n: len(where) for n, (what, *where) in enumerate(RS_ORDER) if what == 2}

    def backward(chunks):
        lhs = jnp.concatenate([dt[j] for j in range(NY)], axis=1)
        for zi, xi in chunks:
            tc = col_of(zi, xi, 1)
            rhs = jnp.concatenate([tile_pair((y - j + NY) % NY, tc) for j in range(NY)], axis=0)
            both = jnp.dot(lhs, rhs, preferred_element_type=F32)
            own32[zi, xi] = both[:, :tile]
            sibsend[zi, xi] = both[:, tile:].astype(BF16)
        for zi, xi in chunks:
            send(("rss", back_batch[zi, xi]), "rs", sibsend.at[zi, xi], sibrecv.at[zi, xi], sibling)

    parent = {}
    for p, (kind, _, _) in enumerate(PARTS):
        for zi in range(NZ):
            for xi in range(NX):
                for axis, (zd, xd), hops, pair in children(kind, zi, xi):
                    parent[zd, xd, p] = (axis, hops, pair)

    waited = set()

    def once(name, dst):
        if name not in waited:
            waited.add(name)
            arrived(name, dst)

    def rs_piece(zi, xi, p):
        kind, r0, r1 = PARTS[p]
        f = pl.ds(2 * r0, 2 * (r1 - r0))
        n = back_batch[zi, xi]
        once(("rss", n), sibrecv.at[pl.ds(0, back_size[n]), 0])
        below = children(kind, zi, xi)
        for _, (zd, xd), _, _ in below:
            once(("rs", zd, xd, p), landed.at[zd, xd, f])
        total = own32[zi, xi, f] + sibrecv[zi, xi, f].astype(F32)
        for _, (zd, xd), _, pair in below:
            term = landed[zd, xd, f].astype(F32)
            total = total + (term if pair is None else jnp.where(k == pair, term, 0.0))
        if (zi, xi) == (0, 0):
            back_t[f] = total
            return
        own[zi, xi, f] = total.astype(BF16)
        axis, hops, pair = parent[zi, xi, p]
        send(("rs", zi, xi, p), "rs", own.at[zi, xi, f], landed.at[zi, xi, f], toward(axis, hops, pair))

    steps = {at: n + 1 for n, at in enumerate(G_AT)}
    for i, (what, *where) in enumerate(RS_ORDER):
        if what == 0:
            rs_piece(*where)
        else:
            backward(where)
        if i in steps:
            g_step(steps[i])

    gf_out[...] = lax.dot_general(
        back_t[...].T.astype(BF16), weight[...], (((1,), (1,)), ((), ())), preferred_element_type=F32
    ).astype(BF16)
    sent("yd", values.at[pl.ds(0, 4 * (NY - 1))])
    sent("rs", values.at[pl.ds(0, 2 * (2 * NZ * NX - 1))])
    sent("g1", g1r)
    sent("g2", g2r.at[pl.ds(0, NY * NX - 1)])
    sent("g4", g4r.at[pl.ds(0, NZ - 1)])
    sent("g5", g5.at[pl.ds(0, NY * NX - 1)])
    sent("g7", g7.at[0])


COPIES = 149
GROUPS = 8


def on_device(features, weight, bias, cotangent, tile_values, tile_rows, tile_cols, tile_count):
    node_rows, feat = features.shape
    slots, tile = tile_values.shape[2], tile_values.shape[-1]
    half = feat // 2
    blocks = NZ * NX * 2
    scale = float((node_rows * blocks * NY) ** -0.5)
    vmem = pl.BlockSpec(memory_space=pltpu.VMEM)
    act, gf, gw, gb = pl.pallas_call(
        functools.partial(body, tile, slots, scale),
        out_shape=(
            jax.ShapeDtypeStruct((node_rows, feat), BF16),
            jax.ShapeDtypeStruct((node_rows, feat), BF16),
            jax.ShapeDtypeStruct((feat, feat), F32),
            jax.ShapeDtypeStruct((1, feat), F32),
        ),
        in_specs=[pl.BlockSpec(memory_space=pltpu.HBM)] * 8,
        out_specs=(vmem,) * 4,
        scratch_shapes=[
            pltpu.VMEM((node_rows, feat), BF16),
            pltpu.VMEM((feat, feat), BF16),
            pltpu.VMEM((1, feat), F32),
            pltpu.VMEM((node_rows, feat), BF16),
            pltpu.VMEM((1, 1, slots), jnp.int32),
            pltpu.VMEM((1, 1, slots), jnp.int32),
            pltpu.VMEM((1, 1), jnp.int32),
            pltpu.VMEM((slots + 1, tile, tile), BF16),
            pltpu.VMEM((8, 128), jnp.int32),
            pltpu.SMEM((8, 128), jnp.int32),
            pltpu.VMEM((NZ, NX, 2, node_rows, feat), BF16),
            pltpu.VMEM((NY * node_rows, feat), F32),
            pltpu.VMEM((NY, node_rows, feat), BF16),
            pltpu.VMEM((NY, node_rows, feat), BF16),
            pltpu.VMEM((NY, feat, node_rows), BF16),
            pltpu.VMEM((NZ, NX, feat, tile), F32),
            pltpu.VMEM((NZ, NX, feat, tile), BF16),
            pltpu.VMEM((NZ, NX, feat, tile), BF16),
            pltpu.VMEM((NZ, NX, feat, tile), BF16),
            pltpu.VMEM((NZ, NX, feat, tile), BF16),
            pltpu.VMEM((feat, tile), F32),
            pltpu.VMEM((2, half + 8, feat), F32),
            pltpu.VMEM((half + 8, feat), F32),
            pltpu.VMEM((NY * NX, 16, feat), F32),
            pltpu.VMEM((NY * NX, 16, feat), F32),
            pltpu.VMEM((NZ, 16, feat), F32),
            pltpu.VMEM((NY * NX, 8, feat), F32),
            pltpu.VMEM((2, half, feat), F32),
            pltpu.SemaphoreType.DMA((GROUPS,)),
            pltpu.SemaphoreType.DMA((COPIES,)),
            pltpu.SemaphoreType.DMA((9,)),
        ],
        compiler_params=pltpu.CompilerParams(
            collective_id=0, has_side_effects=True, vmem_limit_bytes=64 * 1024 * 1024
        ),
        cost_estimate=pl.CostEstimate(
            flops=4 * NY * node_rows * blocks * node_rows * feat,
            bytes_accessed=slots * tile * tile * 2,
            transcendentals=node_rows * feat,
        ),
    )(features, weight, bias.reshape(1, feat), cotangent, tile_values, tile_rows, tile_cols, tile_count)
    return act, gf, gw, gb.reshape(feat)


def solution(mesh):
    in_specs = (
        P(("row", "rep"), None),
        P(),
        P(),
        P(("row", "rep"), None),
        P("row", "rep", None, None, None),
        P("row", "rep", None),
        P("row", "rep", None),
        P("row", "rep"),
    )
    out_specs = (P(("row", "rep"), None), P(("row", "rep"), None), P(), P())
    return jax.shard_map(
        on_device, mesh=mesh, in_specs=in_specs, out_specs=out_specs, check_vma=False
    )
```

```python
import functools

import jax
import jax.numpy as jnp
from jax import lax
from jax.experimental import pallas as pl
from jax.experimental.pallas import tpu as pltpu
from jax.sharding import PartitionSpec as P

MESH = pl.DeviceIdType.MESH
F32 = jnp.float32
BF16 = jnp.bfloat16
NZ, NX, NY = 8, 4, 4
AG_SCHEMES = (
    ({0: ((3, 2), (4, -2), (1, 1), (2, -1)), 3: ((5, 1),), 4: ((6, -1),)}, (3, 4), 7, 2),
    ({0: ((3, 2), (1, 1), (2, -1))}, (), 0, 0),
    ({0: ((1, 1), (2, -1))}, (1, 2), 3, 1),
    ({0: ((3, 2), (4, -2), (1, 1), (2, -1)), 3: ((5, 1),), 4: ((6, -1),)}, (3, 4), 7, 2),
)
RS_SCHEMES = (
    ({0: ((3, 2), (4, -2), (1, 1), (2, -1)), 3: ((5, 1),), 4: ((6, -1),)}, (3, 4), 7, 2),
    ({0: ((3, 2), (1, 1), (2, -1))}, (), 0, 0),
    ({0: ((1, 1), (2, -1))}, (1, 2), 3, 1),
    ({0: ((3, 2), (4, -2), (1, 1), (2, -1)), 3: ((5, 1),), 4: ((6, -1),)}, (3, 4), 7, 2),
)
Z_REACH, X_REACH = ((1, 2), (1, 2))
AG_PARTS = ((1, 0, 96), (2, 96, 128))
RS_PARTS = ((1, 0, 96), (2, 96, 128))
AG_ORDER = (
    (0,0,0,0), (0,0,0,1), (1,0,0), (0,0,3,0), (0,3,0,0), (0,4,0,0), (0,0,1,0), (0,0,2,0), (0,1,0,0), (0,0,3,1),
    (0,2,0,0), (1,0,3), (0,0,2,1), (0,0,1,1), (1,0,2), (1,0,1), (0,3,0,1), (0,4,0,1), (1,3,0), (1,4,0), (0,1,0,1),
    (0,2,0,1), (1,1,0), (1,2,0), (2,(0,0),(0,3)), (0,3,1,0), (0,3,2,0), (2,(0,2),(0,1)), (0,5,0,0), (2,(3,0),(4,0)),
    (0,4,1,0), (0,4,2,0), (2,(1,0),(2,0)), (0,7,0,0), (0,1,1,0), (0,1,2,0), (0,3,3,1), (0,6,0,0), (0,1,3,1),
    (0,2,1,0), (0,2,2,0), (0,3,3,0), (1,3,3), (0,4,3,1), (0,3,2,1), (0,2,3,1), (1,3,2), (0,1,2,1), (1,1,2), (0,5,1,0),
    (0,5,2,0), (0,4,2,1), (1,4,2), (0,4,3,0), (1,4,3), (2,(3,3),(3,2)), (0,3,1,1), (0,2,2,1), (1,3,1), (1,2,2),
    (0,1,1,1), (1,1,1), (0,5,0,1), (1,5,0), (0,7,1,0), (0,7,2,0), (2,(1,2),(4,2)), (0,4,1,1), (1,4,1), (0,1,3,0),
    (0,2,1,1), (1,1,3), (1,2,1), (2,(4,3),(3,1)), (2,(2,2),(1,1)), (0,7,0,1), (1,7,0), (0,6,1,0), (0,6,2,0),
    (0,5,3,1), (0,6,0,1), (1,6,0), (2,(5,0),(4,1)), (0,2,3,0), (1,2,3), (0,7,3,1), (2,(1,3),(2,1)), (0,5,3,0),
    (1,5,3), (0,5,2,1), (0,6,3,1), (1,5,2), (0,7,3,0), (1,7,3), (2,(7,0),(6,0)), (0,7,2,1), (1,7,2), (2,(2,3),(5,3)),
    (0,6,3,0), (0,5,1,1), (0,6,2,1), (1,6,3), (1,5,1), (1,6,2), (2,(5,2),(7,3)), (0,7,1,1), (1,7,1), (0,6,1,1),
    (1,6,1), (2,(7,2),(6,3)), (2,(5,1),(6,2)), (2,(7,1),(6,1)),
)
RS_ORDER = (
    (2,(7,3),(5,3)), (2,(6,3),(7,1)), (2,(7,2),(5,1)), (2,(6,1),(6,2)), (2,(5,2),(4,3)), (2,(3,3),(1,3)), (0,7,3,0),
    (0,7,3,1), (0,5,3,0), (0,5,3,1), (0,6,3,0), (0,6,3,1), (2,(2,3),(7,0)), (0,7,1,1), (0,7,2,1), (2,(5,0),(6,0)),
    (0,5,1,1), (2,(3,1),(4,1)), (0,6,1,1), (0,6,2,1), (2,(4,2),(3,2)), (0,5,2,1), (2,(2,1),(1,1)), (0,4,3,0),
    (0,3,3,0), (2,(2,2),(1,2)), (0,1,3,0), (0,7,1,0), (0,7,2,0), (0,2,3,0), (0,7,0,1), (0,1,3,1), (0,5,1,0),
    (0,5,2,0), (0,3,3,1), (0,4,3,1), (0,2,3,1), (0,6,1,0), (0,6,2,0), (0,5,0,1), (0,6,0,1), (2,(4,0),(3,0)),
    (2,(0,3),(1,0)), (0,2,1,1), (0,4,1,0), (0,4,2,0), (0,1,1,1), (2,(2,0),(0,1)), (0,2,2,1), (0,3,1,0), (0,3,2,0),
    (0,1,2,1), (0,3,1,1), (0,4,1,1), (0,1,1,0), (0,4,2,1), (0,3,2,1), (0,1,2,0), (0,0,3,0), (0,1,0,1),
    (2,(0,2),(0,0)), (0,2,0,1), (0,7,0,0), (0,0,1,0), (0,2,1,0), (0,2,2,0), (0,0,2,0), (0,0,3,1), (0,5,0,0),
    (0,4,0,1), (0,3,0,1), (0,6,0,0), (0,0,1,1), (0,0,2,1), (0,1,0,0), (0,3,0,0), (0,4,0,0), (0,2,0,0), (0,0,0,1),
    (0,0,0,0),
)
G_AT = (40, 72, 77, 79)


def moves(schemes, kind, zi, xi):
    z_column, x_row, x_first, z_second = schemes
    if kind == 1:
        if xi == 0:
            yield "z", zi, z_column
        yield "x", xi, (x_first if zi else x_row)
    else:
        if zi == 0:
            yield "x", xi, x_row
        yield "z", zi, (z_second if xi else z_column)


def children(schemes, kind, zi, xi):
    found = []
    for axis, at, (steps, pair, last, hops) in moves(schemes, kind, zi, xi):
        for to, h in steps.get(at, ()):
            found.append((axis, (to, xi) if axis == "z" else (zi, to), h, None))
        if at in pair:
            found.append((axis, (last, xi) if axis == "z" else (zi, last), hops, pair.index(at)))
    return found


def body(
    tile, slots, scale,
    features_hbm, weight_hbm, bias_hbm, cotangent_hbm, values_hbm, rows_hbm, cols_hbm, count_hbm,
    act_out, gf_out, gw_out, gb_out,
    features, weight, bias, cotangent, rows, cols, count,
    values, inverse_v, inverse, gathered, acc, ysend, yrecv, dt,
    own32, own, sibsend, sibrecv, landed, back_t,
    g1s, g1r, g2s, g2r, g4r, g5, g7,
    send_sem, recv_sem, local_sem,
):
    r = lax.axis_index("row")
    y = lax.axis_index("rep")
    z = r // (2 * NX)
    x = (r // 2) % NX
    k = r % 2
    node_rows, feat = features_hbm.shape
    half = feat // 2

    def at(zz, xx, kk, yy):
        return ((zz * NX + xx) * 2 + kk, yy)

    def z_off(d):
        return at((z + d + NZ) % NZ, x, k, y)

    def x_off(d):
        return at(z, (x + d + NX) % NX, k, y)

    def y_off(d):
        return at(z, x, k, (y + d + NY) % NY)

    def toward(axis, hops, pair):
        d = hops if pair is None else hops * (1 - 2 * k)
        return z_off(d) if axis == "z" else x_off(d)

    sibling = at(z, x, 1 - k, y)
    names = {}
    groups = {}

    def copy(name, group, src, dst, device):
        i = names.setdefault(name, len(names))
        j = groups.setdefault(group, len(groups))
        return pltpu.make_async_remote_copy(
            src_ref=src, dst_ref=dst, send_sem=send_sem.at[j], recv_sem=recv_sem.at[i],
            device_id=device, device_id_type=MESH,
        )

    def send(name, group, src, dst, device):
        copy(name, group, src, dst, device).start()

    def arrived(name, dst):
        copy(name, "ag", dst, dst, sibling).wait_recv()

    def sent(group, src):
        copy("y", group, src, src, sibling).wait_send()

    loads = [
        pltpu.make_async_copy(src, dst, local_sem.at[n])
        for n, (src, dst) in enumerate((
            (features_hbm, features), (rows_hbm, rows), (cols_hbm, cols), (count_hbm, count),
            (weight_hbm, weight), (bias_hbm, bias), (cotangent_hbm, cotangent),
            (values_hbm.at[0, 0], values.at[pl.ds(0, slots)]),
        ))
    ]
    for load in loads:
        load.start()
    barrier = pltpu.get_barrier_semaphore()
    peers = (
        [z_off(s * d) for d in Z_REACH for s in (1, -1)]
        + [x_off(s * d) for d in X_REACH for s in (1, -1)]
        + [y_off(d) for d in range(1, NY)]
        + [sibling]
    )
    for p in peers:
        pl.semaphore_signal(barrier, inc=1, device_id=p, device_id_type=MESH)
    loads[0].wait()
    pl.semaphore_wait(barrier, len(peers))

    seen = set()

    def ag_piece(zi, xi, p):
        kind, r0, r1 = AG_PARTS[p]
        part = pl.ds(r0, r1 - r0)
        if (zi, xi) == (0, 0):
            source = features.at[part]
        else:
            source = gathered.at[zi, xi, 0, part]
            arrived(("ag", zi, xi, p), source)
        for axis, (zd, xd), hops, pair in children(AG_SCHEMES, kind, zi, xi):
            origin = source
            if pair is not None:
                if (zd, xd, p) not in seen:
                    seen.add((zd, xd, p))
                    continue
                if axis == "z":
                    origin = gathered.at[zi - pair + k, xi, 0, part]
                else:
                    origin = gathered.at[zi, xi - pair + k, 0, part]
            send(("ag", zd, xd, p), "ag", origin, gathered.at[zd, xd, 0, part], toward(axis, hops, pair))

    batch_of = {c: n for n, (what, *where) in enumerate(AG_ORDER) if what == 2 for c in where}

    def ag_share(zi, xi):
        source = features if (zi, xi) == (0, 0) else gathered.at[zi, xi, 0]
        send(("share", batch_of[zi, xi]), "ag", source, gathered.at[zi, xi, 1], sibling)

    def offset_of(slot):
        return (slot + 1) // 2 * (2 * (slot % 2) - 1)

    def tile_of(tr, tc):
        p = tr * (NZ * NX * 2) + tc
        return values[inverse[p // 128, p % 128]]

    def tile_pair(tr, tc_own):
        return jnp.concatenate([tile_of(tr, tc_own), tile_of(tr, tc_own + 1 - 2 * k)], axis=1)

    def col_of(zi, xi, sign):
        zz = (z + sign * offset_of(zi) + NZ) % NZ
        xx = (x + sign * offset_of(xi) + NX) % NX
        return (zz * NX + xx) * 2 + k

    def forward(chunks):
        arrived(("share", batch_of[chunks[0]]), gathered.at[pl.ds(0, len(chunks)), 0, 1])
        lhs = jnp.concatenate([
            jnp.concatenate([tile_pair((y + j) % NY, col_of(zi, xi, -1)) for zi, xi in chunks], axis=1)
            for j in range(NY)
        ], axis=0)
        rhs = jnp.concatenate([gathered[zi, xi].reshape(2 * node_rows, feat) for zi, xi in chunks], axis=0)
        term = jnp.dot(lhs, rhs, preferred_element_type=F32)
        if (0, 0) in chunks:
            acc[...] = term
        else:
            acc[...] += term

    todo = list(AG_ORDER)
    while todo[0][:3] == (0, 0, 0):
        ag_piece(*todo.pop(0)[1:])
    gathered[0, 0, 0] = features[...]

    for load in loads[1:4]:
        load.wait()
    key = jnp.where(
        lax.broadcasted_iota(jnp.int32, (1, slots), 1) < count[...],
        rows[0] * (NZ * NX * 2) + cols[0], -1,
    )
    best = [jnp.full((1, 128), slots, jnp.int32) for _ in range(2)]
    for k0 in range(0, slots, 128):
        n = min(128, slots - k0)
        part = key[:, k0:k0 + n]
        if n < 128:
            part = jnp.concatenate([part, jnp.full((1, 128 - n), -1, jnp.int32)], axis=1)
        column = jnp.broadcast_to(part, (128, 128)).T
        slot = lax.broadcasted_iota(jnp.int32, (128, 128), 0) + k0
        for h in range(2):
            place = lax.broadcasted_iota(jnp.int32, (128, 128), 1) + h * 128
            hit = jnp.where(column == place, slot, slots)
            best[h] = jnp.minimum(best[h], jnp.min(hit, axis=0, keepdims=True))
    inverse_v[...] = jnp.concatenate(best + [jnp.full((6, 128), slots, jnp.int32)], axis=0)
    to_smem = pltpu.make_async_copy(inverse_v, inverse, local_sem.at[len(loads)])
    to_smem.start()
    values[slots] = jnp.zeros((tile, tile), BF16)

    ready = False
    for what, *where in todo:
        if what == 0:
            ag_piece(*where)
        elif what == 1:
            ag_share(*where)
        else:
            if not ready:
                to_smem.wait()
                for load in loads[4:]:
                    load.wait()
                ready = True
            forward(where)

    for j in (2, 1, 3):
        ysend[j] = acc[pl.ds(j * node_rows, node_rows)].astype(BF16)
        send("y", "yd", ysend.at[j], yrecv.at[j], y_off(j))
    agg = acc[pl.ds(0, node_rows)]
    arrived("y", yrecv.at[pl.ds(1, 3)])
    for j in (1, 3, 2):
        agg = agg + yrecv[j].astype(F32)
    agg_hi = agg.astype(BF16)
    agg_lo = (agg - agg_hi.astype(F32)).astype(BF16)
    halves = []
    for h in range(2):
        f = pl.ds(h * half, half)
        pre = (
            jnp.dot(agg_hi, weight[:, f], preferred_element_type=F32)
            + jnp.dot(agg_lo, weight[:, f], preferred_element_type=F32)
            + bias[:, f]
        )
        sig = jax.nn.sigmoid(pre)
        dpre = (cotangent[:, f].astype(F32) * sig * (1.0 + pre * (1.0 - sig))).astype(BF16)
        dt[0, f] = dpre.astype(F32).T.astype(BF16)
        for j in (2, 1, 3):
            send(("d", h), "yd", dt.at[0, f], dt.at[j, f], y_off(j))
        act_out[:, f] = (pre * sig).astype(BF16)
        halves.append(dpre)
    dpre = jnp.concatenate(halves, axis=1)

    aggt_hi = agg_hi.astype(F32).T.astype(BF16)
    aggt_lo = agg_lo.astype(F32).T.astype(BF16)
    bias_row = jnp.sum(dpre.astype(F32), axis=0, keepdims=True)
    bias_rows = jnp.concatenate([bias_row, jnp.zeros((7, feat), F32)], axis=0)
    gw = jnp.dot(aggt_hi, dpre, preferred_element_type=F32) + jnp.dot(
        aggt_lo, dpre, preferred_element_type=F32
    )
    for h in range(2):
        g1s[h, pl.ds(0, half)] = gw[h * half:(h + 1) * half]
        g1s[h, pl.ds(half, 8)] = bias_rows
    send("g1", "g1", g1s.at[1 - k], g1r, sibling)

    q = y * NX + x
    square = [(dy, dx) for dy in (2, 1, 3, 0) for dx in (2, 1, 3, 0) if (dy, dx) != (0, 0)]

    def in_square(dy, dx):
        yy, xx = (y + dy) % NY, (x + dx) % NX
        return yy * NX + xx, at(z, xx, k, yy)

    def g_step(n):
        if n == 0:
            arrived("g1", g1r)
            total = g1s[k] + g1r[...]
            for c in range(NY * NX):
                g2s[c, pl.ds(0, 8)] = total[c * 8:(c + 1) * 8]
                g2s[c, pl.ds(8, 8)] = total[half:half + 8]
            for dy, dx in square:
                c, device = in_square(dy, dx)
                send("g2", "g2", g2s.at[c], g2r.at[q], device)
            g2r[q] = g2s[q]
        elif n == 1:
            arrived("g2", g2r.at[pl.ds(0, NY * NX - 1)])
            total = g2r[0]
            for c in range(1, NY * NX):
                total = total + g2r[c]
            g4r[z] = total
            for j in (4, 3, 5, 2, 6, 1, 7):
                send("g4", "g4", g4r.at[z], g4r.at[z], z_off(j))
        elif n == 2:
            arrived("g4", g4r.at[pl.ds(0, NZ - 1)])
            total = g4r[0]
            for j in range(1, NZ):
                total = total + g4r[j]
            total = total * scale
            gb_out[...] = total[8:9]
            g5[q] = total[0:8]
            for dy, dx in square:
                send("g5", "g5", g5.at[q], g5.at[q], in_square(dy, dx)[1])
        elif n == 3:
            arrived("g5", g5.at[pl.ds(0, NY * NX - 1)])
            g7[k] = g5[...].reshape(half, feat)
            send("g7", "g7", g7.at[k], g7.at[k], sibling)
        elif n == 4:
            arrived("g7", g7.at[1 - k])
            gw_out[...] = g7[...].reshape(feat, feat)

    g_step(0)
    sent("ag", values.at[pl.ds(0, 2 * (2 * NZ * NX - 1))])

    for h in range(2):
        arrived(("d", h), dt.at[pl.ds(1, NY - 1), pl.ds(h * half, half)])

    back_batch = {c: n for n, (what, *where) in enumerate(RS_ORDER) if what == 2 for c in where}
    back_size = {n: len(where) for n, (what, *where) in enumerate(RS_ORDER) if what == 2}

    def backward(chunks):
        lhs = jnp.concatenate([dt[j] for j in range(NY)], axis=1)
        for zi, xi in chunks:
            tc = col_of(zi, xi, 1)
            rhs = jnp.concatenate([tile_pair((y - j + NY) % NY, tc) for j in range(NY)], axis=0)
            both = jnp.dot(lhs, rhs, preferred_element_type=F32)
            own32[zi, xi] = both[:, :tile]
            sibsend[zi, xi] = both[:, tile:].astype(BF16)
        for zi, xi in chunks:
            send(("rss", back_batch[zi, xi]), "rs", sibsend.at[zi, xi], sibrecv.at[zi, xi], sibling)

    parent = {}
    for p, (kind, _, _) in enumerate(RS_PARTS):
        for zi in range(NZ):
            for xi in range(NX):
                for axis, (zd, xd), hops, pair in children(RS_SCHEMES, kind, zi, xi):
                    parent[zd, xd, p] = (axis, hops, pair)

    waited = set()

    def once(name, dst):
        if name not in waited:
            waited.add(name)
            arrived(name, dst)

    def rs_piece(zi, xi, p):
        kind, r0, r1 = RS_PARTS[p]
        f = pl.ds(2 * r0, 2 * (r1 - r0))
        n = back_batch[zi, xi]
        once(("rss", n), sibrecv.at[pl.ds(0, back_size[n]), 0])
        below = children(RS_SCHEMES, kind, zi, xi)
        for _, (zd, xd), _, _ in below:
            once(("rs", zd, xd, p), landed.at[zd, xd, f])
        total = own32[zi, xi, f] + sibrecv[zi, xi, f].astype(F32)
        for _, (zd, xd), _, pair in below:
            term = landed[zd, xd, f].astype(F32)
            total = total + (term if pair is None else jnp.where(k == pair, term, 0.0))
        if (zi, xi) == (0, 0):
            back_t[f] = total
            return
        own[zi, xi, f] = total.astype(BF16)
        axis, hops, pair = parent[zi, xi, p]
        send(("rs", zi, xi, p), "rs", own.at[zi, xi, f], landed.at[zi, xi, f], toward(axis, hops, pair))

    steps = {at: n + 1 for n, at in enumerate(G_AT)}
    for i, (what, *where) in enumerate(RS_ORDER):
        if what == 0:
            rs_piece(*where)
        else:
            backward(where)
        if i in steps:
            g_step(steps[i])

    gf_out[...] = lax.dot_general(
        back_t[...].T.astype(BF16), weight[...], (((1,), (1,)), ((), ())), preferred_element_type=F32
    ).astype(BF16)
    sent("yd", values.at[pl.ds(0, 4 * (NY - 1))])
    sent("rs", values.at[pl.ds(0, 2 * (2 * NZ * NX - 1))])
    sent("g1", g1r)
    sent("g2", g2r.at[pl.ds(0, NY * NX - 1)])
    sent("g4", g4r.at[pl.ds(0, NZ - 1)])
    sent("g5", g5.at[pl.ds(0, NY * NX - 1)])
    sent("g7", g7.at[0])


COPIES = 164
GROUPS = 8


def hand_over(*refs):
    count = 4
    ins, outs, held, sems = refs[:count], refs[count:2 * count], refs[2 * count:3 * count], refs[-1]
    first = [pltpu.make_async_copy(ins[n], held[n], sems.at[0, n]) for n in range(count)]
    second = [pltpu.make_async_copy(held[n], outs[n], sems.at[1, n]) for n in range(count)]
    for c in first:
        c.start()
    for c, d in zip(first, second):
        c.wait()
        d.start()
    for d in second:
        d.wait()


def on_device(features, weight, bias, cotangent, tile_values, tile_rows, tile_cols, tile_count):
    node_rows, feat = features.shape
    slots, tile = tile_values.shape[2], tile_values.shape[-1]
    half = feat // 2
    blocks = NZ * NX * 2
    scale = float((node_rows * blocks * NY) ** -0.5)
    vmem = pl.BlockSpec(memory_space=pltpu.VMEM)
    act, gf, gw, gb = pl.pallas_call(
        functools.partial(body, tile, slots, scale),
        out_shape=(
            jax.ShapeDtypeStruct((node_rows, feat), BF16),
            jax.ShapeDtypeStruct((node_rows, feat), BF16),
            jax.ShapeDtypeStruct((feat, feat), F32),
            jax.ShapeDtypeStruct((1, feat), F32),
        ),
        in_specs=[pl.BlockSpec(memory_space=pltpu.HBM)] * 8,
        out_specs=(vmem,) * 4,
        scratch_shapes=[
            pltpu.VMEM((node_rows, feat), BF16),
            pltpu.VMEM((feat, feat), BF16),
            pltpu.VMEM((1, feat), F32),
            pltpu.VMEM((node_rows, feat), BF16),
            pltpu.VMEM((1, 1, slots), jnp.int32),
            pltpu.VMEM((1, 1, slots), jnp.int32),
            pltpu.VMEM((1, 1), jnp.int32),
            pltpu.VMEM((slots + 1, tile, tile), BF16),
            pltpu.VMEM((8, 128), jnp.int32),
            pltpu.SMEM((8, 128), jnp.int32),
            pltpu.VMEM((NZ, NX, 2, node_rows, feat), BF16),
            pltpu.VMEM((NY * node_rows, feat), F32),
            pltpu.VMEM((NY, node_rows, feat), BF16),
            pltpu.VMEM((NY, node_rows, feat), BF16),
            pltpu.VMEM((NY, feat, node_rows), BF16),
            pltpu.VMEM((NZ, NX, feat, tile), F32),
            pltpu.VMEM((NZ, NX, feat, tile), BF16),
            pltpu.VMEM((NZ, NX, feat, tile), BF16),
            pltpu.VMEM((NZ, NX, feat, tile), BF16),
            pltpu.VMEM((NZ, NX, feat, tile), BF16),
            pltpu.VMEM((feat, tile), F32),
            pltpu.VMEM((2, half + 8, feat), F32),
            pltpu.VMEM((half + 8, feat), F32),
            pltpu.VMEM((NY * NX, 16, feat), F32),
            pltpu.VMEM((NY * NX, 16, feat), F32),
            pltpu.VMEM((NZ, 16, feat), F32),
            pltpu.VMEM((NY * NX, 8, feat), F32),
            pltpu.VMEM((2, half, feat), F32),
            pltpu.SemaphoreType.DMA((GROUPS,)),
            pltpu.SemaphoreType.DMA((COPIES,)),
            pltpu.SemaphoreType.DMA((9,)),
        ],
        compiler_params=pltpu.CompilerParams(
            collective_id=0, has_side_effects=True, vmem_limit_bytes=64 * 1024 * 1024
        ),
        cost_estimate=pl.CostEstimate(
            flops=4 * NY * node_rows * blocks * node_rows * feat,
            bytes_accessed=slots * tile * tile * 2,
            transcendentals=node_rows * feat,
        ),
    )(features, weight, bias.reshape(1, feat), cotangent, tile_values, tile_rows, tile_cols, tile_count)
    hbm = pl.BlockSpec(memory_space=pltpu.HBM)
    results = (act, gf, gw, gb)
    act, gf, gw, gb = pl.pallas_call(
        hand_over,
        out_shape=tuple(jax.ShapeDtypeStruct(a.shape, a.dtype) for a in results),
        in_specs=[hbm] * 4,
        out_specs=(hbm,) * 4,
        scratch_shapes=[pltpu.VMEM(a.shape, a.dtype) for a in results] + [pltpu.SemaphoreType.DMA((2, 4))],
        compiler_params=pltpu.CompilerParams(vmem_limit_bytes=64 * 1024 * 1024),
    )(*results)
    return act, gf, gw, gb.reshape(feat)


def solution(mesh):
    in_specs = (
        P(("row", "rep"), None),
        P(),
        P(),
        P(("row", "rep"), None),
        P("row", "rep", None, None, None),
        P("row", "rep", None),
        P("row", "rep", None),
        P("row", "rep"),
    )
    out_specs = (P(("row", "rep"), None), P(("row", "rep"), None), P(), P())
    return jax.shard_map(
        on_device, mesh=mesh, in_specs=in_specs, out_specs=out_specs, check_vma=False
    )
```

```python
import functools

import jax
import jax.numpy as jnp
from jax import lax
from jax.experimental import pallas as pl
from jax.experimental.pallas import tpu as pltpu
from jax.sharding import PartitionSpec as P

MESH = pl.DeviceIdType.MESH
F32 = jnp.float32
BF16 = jnp.bfloat16
NZ, NX, NY = 8, 4, 4
AG_SCHEMES = (
    ({0: ((3, 2), (4, -2), (1, 1), (2, -1)), 3: ((5, 1),), 4: ((6, -1),)}, (3, 4), 7, 2),
    ({0: ((3, 2), (1, 1), (2, -1))}, (), 0, 0),
    ({0: ((1, 1), (2, -1))}, (1, 2), 3, 1),
    ({0: ((3, 2), (4, -2), (1, 1), (2, -1)), 3: ((5, 1),), 4: ((6, -1),)}, (3, 4), 7, 2),
)
RS_SCHEMES = (
    ({0: ((3, 2), (4, -2), (1, 1), (2, -1)), 3: ((5, 1),), 4: ((6, -1),)}, (3, 4), 7, 2),
    ({0: ((3, 2), (1, 1), (2, -1))}, (), 0, 0),
    ({0: ((1, 1), (2, -1))}, (1, 2), 3, 1),
    ({0: ((3, 2), (4, -2), (1, 1), (2, -1)), 3: ((5, 1),), 4: ((6, -1),)}, (3, 4), 7, 2),
)
Z_REACH, X_REACH = ((1, 2), (1, 2))
AG_PARTS = ((1, 0, 96), (2, 96, 128))
RS_PARTS = ((1, 0, 96), (2, 96, 128))
AG_ORDER = (
    (0,0,0,0), (0,0,0,1), (1,0,0), (0,0,3,0), (0,3,0,0), (0,4,0,0), (0,0,1,0), (0,0,2,0), (0,1,0,0), (0,0,3,1),
    (0,2,0,0), (1,0,3), (0,0,2,1), (0,0,1,1), (1,0,2), (1,0,1), (0,3,0,1), (0,4,0,1), (1,3,0), (1,4,0), (0,1,0,1),
    (0,2,0,1), (1,1,0), (1,2,0), (2,(0,0),(0,3)), (0,3,1,0), (0,3,2,0), (2,(0,2),(0,1)), (0,5,0,0), (2,(3,0),(4,0)),
    (0,4,1,0), (0,4,2,0), (2,(1,0),(2,0)), (0,7,0,0), (0,1,1,0), (0,1,2,0), (0,3,3,1), (0,6,0,0), (0,1,3,1),
    (0,2,1,0), (0,2,2,0), (0,3,3,0), (1,3,3), (0,4,3,1), (0,3,2,1), (0,2,3,1), (1,3,2), (0,1,2,1), (1,1,2), (0,5,1,0),
    (0,5,2,0), (0,4,2,1), (1,4,2), (0,4,3,0), (1,4,3), (2,(3,3),(3,2)), (0,3,1,1), (0,2,2,1), (1,3,1), (1,2,2),
    (0,1,1,1), (1,1,1), (0,5,0,1), (1,5,0), (0,7,1,0), (0,7,2,0), (2,(1,2),(4,2)), (0,4,1,1), (1,4,1), (0,1,3,0),
    (0,2,1,1), (1,1,3), (1,2,1), (2,(4,3),(3,1)), (2,(2,2),(1,1)), (0,7,0,1), (1,7,0), (0,6,1,0), (0,6,2,0),
    (0,5,3,1), (0,6,0,1), (1,6,0), (2,(5,0),(4,1)), (0,2,3,0), (1,2,3), (0,7,3,1), (2,(1,3),(2,1)), (0,5,3,0),
    (1,5,3), (0,5,2,1), (0,6,3,1), (1,5,2), (0,7,3,0), (1,7,3), (2,(7,0),(6,0)), (0,7,2,1), (1,7,2), (2,(2,3),(5,3)),
    (0,6,3,0), (0,5,1,1), (0,6,2,1), (1,6,3), (1,5,1), (1,6,2), (2,(5,2),(7,3)), (0,7,1,1), (1,7,1), (0,6,1,1),
    (1,6,1), (2,(7,2),(6,3)), (2,(5,1),(6,2)), (2,(7,1),(6,1)),
)
RS_ORDER = (
    (2,(7,3),(5,3)), (2,(6,3),(7,1)), (2,(7,2),(5,1)), (2,(6,1),(6,2)), (2,(5,2),(4,3)), (2,(3,3),(1,3)), (0,7,3,0),
    (0,7,3,1), (0,5,3,0), (0,5,3,1), (0,6,3,0), (0,6,3,1), (2,(2,3),(7,0)), (0,7,1,1), (0,7,2,1), (2,(5,0),(6,0)),
    (0,5,1,1), (2,(3,1),(4,1)), (0,6,1,1), (0,6,2,1), (2,(4,2),(3,2)), (0,5,2,1), (2,(2,1),(1,1)), (0,4,3,0),
    (0,3,3,0), (2,(2,2),(1,2)), (0,1,3,0), (0,7,1,0), (0,7,2,0), (0,2,3,0), (0,7,0,1), (0,1,3,1), (0,5,1,0),
    (0,5,2,0), (0,3,3,1), (0,4,3,1), (0,2,3,1), (0,6,1,0), (0,6,2,0), (0,5,0,1), (0,6,0,1), (2,(4,0),(3,0)),
    (2,(0,3),(1,0)), (0,2,1,1), (0,4,1,0), (0,4,2,0), (0,1,1,1), (2,(2,0),(0,1)), (0,2,2,1), (0,3,1,0), (0,3,2,0),
    (0,1,2,1), (0,3,1,1), (0,4,1,1), (0,1,1,0), (0,4,2,1), (0,3,2,1), (0,1,2,0), (0,0,3,0), (0,1,0,1),
    (2,(0,2),(0,0)), (0,2,0,1), (0,7,0,0), (0,0,1,0), (0,2,1,0), (0,2,2,0), (0,0,2,0), (0,0,3,1), (0,5,0,0),
    (0,4,0,1), (0,3,0,1), (0,6,0,0), (0,0,1,1), (0,0,2,1), (0,1,0,0), (0,3,0,0), (0,4,0,0), (0,2,0,0), (0,0,0,1),
    (0,0,0,0),
)
G_AT = (40, 72, 77, 79)


def moves(schemes, kind, zi, xi):
    z_column, x_row, x_first, z_second = schemes
    if kind == 1:
        if xi == 0:
            yield "z", zi, z_column
        yield "x", xi, (x_first if zi else x_row)
    else:
        if zi == 0:
            yield "x", xi, x_row
        yield "z", zi, (z_second if xi else z_column)


def children(schemes, kind, zi, xi):
    found = []
    for axis, at, (steps, pair, last, hops) in moves(schemes, kind, zi, xi):
        for to, h in steps.get(at, ()):
            found.append((axis, (to, xi) if axis == "z" else (zi, to), h, None))
        if at in pair:
            found.append((axis, (last, xi) if axis == "z" else (zi, last), hops, pair.index(at)))
    return found


def body(
    tile, slots, scale,
    features_hbm, weight_hbm, bias_hbm, cotangent_hbm, values_hbm, rows_hbm, cols_hbm, count_hbm,
    act_out, gf_out, gw_out, gb_out,
    features, weight, bias, cotangent, rows, cols, count,
    values, inverse_v, inverse, gathered, acc, ysend, yrecv, dt,
    own32, own, sibsend, sibrecv, landed, back_t,
    g1s, g1r, g2s, g2r, g4r, g5, g7,
    send_sem, recv_sem, local_sem,
):
    r = lax.axis_index("row")
    y = lax.axis_index("rep")
    z = r // (2 * NX)
    x = (r // 2) % NX
    k = r % 2
    node_rows, feat = features_hbm.shape
    half = feat // 2

    def at(zz, xx, kk, yy):
        return ((zz * NX + xx) * 2 + kk, yy)

    def z_off(d):
        return at((z + d + NZ) % NZ, x, k, y)

    def x_off(d):
        return at(z, (x + d + NX) % NX, k, y)

    def y_off(d):
        return at(z, x, k, (y + d + NY) % NY)

    def toward(axis, hops, pair):
        d = hops if pair is None else hops * (1 - 2 * k)
        return z_off(d) if axis == "z" else x_off(d)

    sibling = at(z, x, 1 - k, y)
    names = {}
    groups = {}

    def copy(name, group, src, dst, device):
        i = names.setdefault(name, len(names))
        j = groups.setdefault(group, len(groups))
        return pltpu.make_async_remote_copy(
            src_ref=src, dst_ref=dst, send_sem=send_sem.at[j], recv_sem=recv_sem.at[i],
            device_id=device, device_id_type=MESH,
        )

    def send(name, group, src, dst, device):
        copy(name, group, src, dst, device).start()

    def arrived(name, dst):
        copy(name, "ag", dst, dst, sibling).wait_recv()

    def sent(group, src):
        copy("y", group, src, src, sibling).wait_send()

    loads = [
        pltpu.make_async_copy(src, dst, local_sem.at[n])
        for n, (src, dst) in enumerate((
            (features_hbm, features), (rows_hbm, rows), (cols_hbm, cols), (count_hbm, count),
            (weight_hbm, weight), (bias_hbm, bias), (cotangent_hbm, cotangent),
            (values_hbm.at[0, 0], values.at[pl.ds(0, slots)]),
        ))
    ]
    for load in loads:
        load.start()
    barrier = pltpu.get_barrier_semaphore()
    peers = (
        [z_off(s * d) for d in Z_REACH for s in (1, -1)]
        + [x_off(s * d) for d in X_REACH for s in (1, -1)]
        + [y_off(d) for d in range(1, NY)]
        + [sibling]
    )
    for p in peers:
        pl.semaphore_signal(barrier, inc=1, device_id=p, device_id_type=MESH)
    loads[0].wait()
    pl.semaphore_wait(barrier, len(peers))

    seen = set()

    def ag_piece(zi, xi, p):
        kind, r0, r1 = AG_PARTS[p]
        part = pl.ds(r0, r1 - r0)
        if (zi, xi) == (0, 0):
            source = features.at[part]
        else:
            source = gathered.at[zi, xi, 0, part]
            arrived(("ag", zi, xi, p), source)
        for axis, (zd, xd), hops, pair in children(AG_SCHEMES, kind, zi, xi):
            origin = source
            if pair is not None:
                if (zd, xd, p) not in seen:
                    seen.add((zd, xd, p))
                    continue
                if axis == "z":
                    origin = gathered.at[zi - pair + k, xi, 0, part]
                else:
                    origin = gathered.at[zi, xi - pair + k, 0, part]
            send(("ag", zd, xd, p), "ag", origin, gathered.at[zd, xd, 0, part], toward(axis, hops, pair))

    batch_of = {c: n for n, (what, *where) in enumerate(AG_ORDER) if what == 2 for c in where}

    def ag_share(zi, xi):
        source = features if (zi, xi) == (0, 0) else gathered.at[zi, xi, 0]
        send(("share", batch_of[zi, xi]), "ag", source, gathered.at[zi, xi, 1], sibling)

    def offset_of(slot):
        return (slot + 1) // 2 * (2 * (slot % 2) - 1)

    def tile_of(tr, tc):
        p = tr * (NZ * NX * 2) + tc
        return values[inverse[p // 128, p % 128]]

    def tile_pair(tr, tc_own):
        return jnp.concatenate([tile_of(tr, tc_own), tile_of(tr, tc_own + 1 - 2 * k)], axis=1)

    def col_of(zi, xi, sign):
        zz = (z + sign * offset_of(zi) + NZ) % NZ
        xx = (x + sign * offset_of(xi) + NX) % NX
        return (zz * NX + xx) * 2 + k

    def forward(chunks):
        arrived(("share", batch_of[chunks[0]]), gathered.at[pl.ds(0, len(chunks)), 0, 1])
        lhs = jnp.concatenate([
            jnp.concatenate([tile_pair((y + j) % NY, col_of(zi, xi, -1)) for zi, xi in chunks], axis=1)
            for j in range(NY)
        ], axis=0)
        rhs = jnp.concatenate([gathered[zi, xi].reshape(2 * node_rows, feat) for zi, xi in chunks], axis=0)
        term = jnp.dot(lhs, rhs, preferred_element_type=F32)
        if (0, 0) in chunks:
            acc[...] = term
        else:
            acc[...] += term

    todo = list(AG_ORDER)
    while todo[0][:3] == (0, 0, 0):
        ag_piece(*todo.pop(0)[1:])
    gathered[0, 0, 0] = features[...]

    for load in loads[1:4]:
        load.wait()
    key = jnp.where(
        lax.broadcasted_iota(jnp.int32, (1, slots), 1) < count[...],
        rows[0] * (NZ * NX * 2) + cols[0], -1,
    )
    best = [jnp.full((1, 128), slots, jnp.int32) for _ in range(2)]
    for k0 in range(0, slots, 128):
        n = min(128, slots - k0)
        part = key[:, k0:k0 + n]
        if n < 128:
            part = jnp.concatenate([part, jnp.full((1, 128 - n), -1, jnp.int32)], axis=1)
        column = jnp.broadcast_to(part, (128, 128)).T
        slot = lax.broadcasted_iota(jnp.int32, (128, 128), 0) + k0
        for h in range(2):
            place = lax.broadcasted_iota(jnp.int32, (128, 128), 1) + h * 128
            hit = jnp.where(column == place, slot, slots)
            best[h] = jnp.minimum(best[h], jnp.min(hit, axis=0, keepdims=True))
    inverse_v[...] = jnp.concatenate(best + [jnp.full((6, 128), slots, jnp.int32)], axis=0)
    to_smem = pltpu.make_async_copy(inverse_v, inverse, local_sem.at[len(loads)])
    to_smem.start()
    values[slots] = jnp.zeros((tile, tile), BF16)

    ready = False
    for what, *where in todo:
        if what == 0:
            ag_piece(*where)
        elif what == 1:
            ag_share(*where)
        else:
            if not ready:
                to_smem.wait()
                for load in loads[4:]:
                    load.wait()
                ready = True
            forward(where)

    for j in (2, 1, 3):
        ysend[j] = acc[pl.ds(j * node_rows, node_rows)].astype(BF16)
        send("y", "yd", ysend.at[j], yrecv.at[j], y_off(j))
    agg = acc[pl.ds(0, node_rows)]
    arrived("y", yrecv.at[pl.ds(1, 3)])
    for j in (1, 3, 2):
        agg = agg + yrecv[j].astype(F32)
    agg_hi = agg.astype(BF16)
    agg_lo = (agg - agg_hi.astype(F32)).astype(BF16)
    halves = []
    for h in range(2):
        f = pl.ds(h * half, half)
        pre = (
            jnp.dot(agg_hi, weight[:, f], preferred_element_type=F32)
            + jnp.dot(agg_lo, weight[:, f], preferred_element_type=F32)
            + bias[:, f]
        )
        sig = jax.nn.sigmoid(pre)
        dpre = (cotangent[:, f].astype(F32) * sig * (1.0 + pre * (1.0 - sig))).astype(BF16)
        dt[0, f] = dpre.astype(F32).T.astype(BF16)
        for j in (2, 1, 3):
            send(("d", h), "yd", dt.at[0, f], dt.at[j, f], y_off(j))
        act_out[:, f] = (pre * sig).astype(BF16)
        halves.append(dpre)
    dpre = jnp.concatenate(halves, axis=1)

    aggt_hi = agg_hi.astype(F32).T.astype(BF16)
    aggt_lo = agg_lo.astype(F32).T.astype(BF16)
    bias_row = jnp.sum(dpre.astype(F32), axis=0, keepdims=True)
    bias_rows = jnp.concatenate([bias_row, jnp.zeros((7, feat), F32)], axis=0)
    gw = jnp.dot(aggt_hi, dpre, preferred_element_type=F32) + jnp.dot(
        aggt_lo, dpre, preferred_element_type=F32
    )
    for h in range(2):
        g1s[h, pl.ds(0, half)] = gw[h * half:(h + 1) * half]
        g1s[h, pl.ds(half, 8)] = bias_rows
    send("g1", "g1", g1s.at[1 - k], g1r, sibling)

    q = y * NX + x
    square = [(dy, dx) for dy in (2, 1, 3, 0) for dx in (2, 1, 3, 0) if (dy, dx) != (0, 0)]

    def in_square(dy, dx):
        yy, xx = (y + dy) % NY, (x + dx) % NX
        return yy * NX + xx, at(z, xx, k, yy)

    def g_step(n):
        if n == 0:
            arrived("g1", g1r)
            total = g1s[k] + g1r[...]
            for c in range(NY * NX):
                g2s[c, pl.ds(0, 8)] = total[c * 8:(c + 1) * 8]
                g2s[c, pl.ds(8, 8)] = total[half:half + 8]
            for dy, dx in square:
                c, device = in_square(dy, dx)
                n_rows = pl.ds(0, 16 if dy == 0 else 8)
                send("g2", "g2", g2s.at[c, n_rows], g2r.at[q, n_rows], device)
            g2r[q] = g2s[q]
        elif n == 1:
            arrived("g2", g2r.at[pl.ds(0, 9)])
            total = g2r[0, pl.ds(0, 8)]
            for c in range(1, NY * NX):
                total = total + g2r[c, pl.ds(0, 8)]
            g4r[z, pl.ds(0, 8)] = total
            total = g2r[y * NX, pl.ds(8, 8)]
            for c in range(1, NX):
                total = total + g2r[y * NX + c, pl.ds(8, 8)]
            g4r[z, pl.ds(8, 8)] = total
            for j in (4, 3, 5, 2, 6, 1, 7):
                send("g4", "g4", g4r.at[z], g4r.at[z], z_off(j))
        elif n == 2:
            arrived("g4", g4r.at[pl.ds(0, NZ - 1)])
            total = g4r[0]
            for j in range(1, NZ):
                total = total + g4r[j]
            g5[q] = total * scale
            for dy, dx in square:
                n_rows = pl.ds(0, 16 if dx == 0 else 8)
                send("g5", "g5", g5.at[q, n_rows], g5.at[q, n_rows], in_square(dy, dx)[1])
        elif n == 3:
            arrived("g5", g5.at[pl.ds(0, 9)])
            g7[k] = g5[:, pl.ds(0, 8)].reshape(half, feat)
            total = g5[x, pl.ds(8, 8)]
            for c in range(1, NY):
                total = total + g5[c * NX + x, pl.ds(8, 8)]
            gb_out[...] = total[0:1]
            send("g7", "g7", g7.at[k], g7.at[k], sibling)
        elif n == 4:
            arrived("g7", g7.at[1 - k])
            gw_out[...] = g7[...].reshape(feat, feat)

    g_step(0)
    sent("ag", values.at[pl.ds(0, 2 * (2 * NZ * NX - 1))])

    for h in range(2):
        arrived(("d", h), dt.at[pl.ds(1, NY - 1), pl.ds(h * half, half)])

    back_batch = {c: n for n, (what, *where) in enumerate(RS_ORDER) if what == 2 for c in where}
    back_size = {n: len(where) for n, (what, *where) in enumerate(RS_ORDER) if what == 2}

    def backward(chunks):
        lhs = jnp.concatenate([dt[j] for j in range(NY)], axis=1)
        for zi, xi in chunks:
            tc = col_of(zi, xi, 1)
            rhs = jnp.concatenate([tile_pair((y - j + NY) % NY, tc) for j in range(NY)], axis=0)
            both = jnp.dot(lhs, rhs, preferred_element_type=F32)
            own32[zi, xi] = both[:, :tile]
            sibsend[zi, xi] = both[:, tile:].astype(BF16)
        for zi, xi in chunks:
            send(("rss", back_batch[zi, xi]), "rs", sibsend.at[zi, xi], sibrecv.at[zi, xi], sibling)

    parent = {}
    for p, (kind, _, _) in enumerate(RS_PARTS):
        for zi in range(NZ):
            for xi in range(NX):
                for axis, (zd, xd), hops, pair in children(RS_SCHEMES, kind, zi, xi):
                    parent[zd, xd, p] = (axis, hops, pair)

    waited = set()

    def once(name, dst):
        if name not in waited:
            waited.add(name)
            arrived(name, dst)

    def rs_piece(zi, xi, p):
        kind, r0, r1 = RS_PARTS[p]
        f = pl.ds(2 * r0, 2 * (r1 - r0))
        n = back_batch[zi, xi]
        once(("rss", n), sibrecv.at[pl.ds(0, back_size[n]), 0])
        below = children(RS_SCHEMES, kind, zi, xi)
        for _, (zd, xd), _, _ in below:
            once(("rs", zd, xd, p), landed.at[zd, xd, f])
        total = own32[zi, xi, f] + sibrecv[zi, xi, f].astype(F32)
        for _, (zd, xd), _, pair in below:
            term = landed[zd, xd, f].astype(F32)
            total = total + (term if pair is None else jnp.where(k == pair, term, 0.0))
        if (zi, xi) == (0, 0):
            back_t[f] = total
            return
        own[zi, xi, f] = total.astype(BF16)
        axis, hops, pair = parent[zi, xi, p]
        send(("rs", zi, xi, p), "rs", own.at[zi, xi, f], landed.at[zi, xi, f], toward(axis, hops, pair))

    steps = {at: n + 1 for n, at in enumerate(G_AT)}
    for i, (what, *where) in enumerate(RS_ORDER):
        if what == 0:
            rs_piece(*where)
        else:
            backward(where)
        if i in steps:
            g_step(steps[i])

    gf_out[...] = lax.dot_general(
        back_t[...].T.astype(BF16), weight[...], (((1,), (1,)), ((), ())), preferred_element_type=F32
    ).astype(BF16)
    sent("yd", values.at[pl.ds(0, 4 * (NY - 1))])
    sent("rs", values.at[pl.ds(0, 2 * (2 * NZ * NX - 1))])
    sent("g1", g1r)
    sent("g2", g2r.at[pl.ds(0, 9)])
    sent("g4", g4r.at[pl.ds(0, NZ - 1)])
    sent("g5", g5.at[pl.ds(0, 9)])
    sent("g7", g7.at[0])


COPIES = 164
GROUPS = 8


def hand_over(*refs):
    count = 4
    ins, outs, held, sems = refs[:count], refs[count:2 * count], refs[2 * count:3 * count], refs[-1]
    first = [pltpu.make_async_copy(ins[n], held[n], sems.at[0, n]) for n in range(count)]
    second = [pltpu.make_async_copy(held[n], outs[n], sems.at[1, n]) for n in range(count)]
    for c in first:
        c.start()
    for c, d in zip(first, second):
        c.wait()
        d.start()
    for d in second:
        d.wait()


def on_device(features, weight, bias, cotangent, tile_values, tile_rows, tile_cols, tile_count):
    node_rows, feat = features.shape
    slots, tile = tile_values.shape[2], tile_values.shape[-1]
    half = feat // 2
    blocks = NZ * NX * 2
    scale = float((node_rows * blocks * NY) ** -0.5)
    vmem = pl.BlockSpec(memory_space=pltpu.VMEM)
    act, gf, gw, gb = pl.pallas_call(
        functools.partial(body, tile, slots, scale),
        out_shape=(
            jax.ShapeDtypeStruct((node_rows, feat), BF16),
            jax.ShapeDtypeStruct((node_rows, feat), BF16),
            jax.ShapeDtypeStruct((feat, feat), F32),
            jax.ShapeDtypeStruct((1, feat), F32),
        ),
        in_specs=[pl.BlockSpec(memory_space=pltpu.HBM)] * 8,
        out_specs=(vmem,) * 4,
        scratch_shapes=[
            pltpu.VMEM((node_rows, feat), BF16),
            pltpu.VMEM((feat, feat), BF16),
            pltpu.VMEM((1, feat), F32),
            pltpu.VMEM((node_rows, feat), BF16),
            pltpu.VMEM((1, 1, slots), jnp.int32),
            pltpu.VMEM((1, 1, slots), jnp.int32),
            pltpu.VMEM((1, 1), jnp.int32),
            pltpu.VMEM((slots + 1, tile, tile), BF16),
            pltpu.VMEM((8, 128), jnp.int32),
            pltpu.SMEM((8, 128), jnp.int32),
            pltpu.VMEM((NZ, NX, 2, node_rows, feat), BF16),
            pltpu.VMEM((NY * node_rows, feat), F32),
            pltpu.VMEM((NY, node_rows, feat), BF16),
            pltpu.VMEM((NY, node_rows, feat), BF16),
            pltpu.VMEM((NY, feat, node_rows), BF16),
            pltpu.VMEM((NZ, NX, feat, tile), F32),
            pltpu.VMEM((NZ, NX, feat, tile), BF16),
            pltpu.VMEM((NZ, NX, feat, tile), BF16),
            pltpu.VMEM((NZ, NX, feat, tile), BF16),
            pltpu.VMEM((NZ, NX, feat, tile), BF16),
            pltpu.VMEM((feat, tile), F32),
            pltpu.VMEM((2, half + 8, feat), F32),
            pltpu.VMEM((half + 8, feat), F32),
            pltpu.VMEM((NY * NX, 16, feat), F32),
            pltpu.VMEM((NY * NX, 16, feat), F32),
            pltpu.VMEM((NZ, 16, feat), F32),
            pltpu.VMEM((NY * NX, 16, feat), F32),
            pltpu.VMEM((2, half, feat), F32),
            pltpu.SemaphoreType.DMA((GROUPS,)),
            pltpu.SemaphoreType.DMA((COPIES,)),
            pltpu.SemaphoreType.DMA((9,)),
        ],
        compiler_params=pltpu.CompilerParams(
            collective_id=0, has_side_effects=True, vmem_limit_bytes=64 * 1024 * 1024
        ),
        cost_estimate=pl.CostEstimate(
            flops=4 * NY * node_rows * blocks * node_rows * feat,
            bytes_accessed=slots * tile * tile * 2,
            transcendentals=node_rows * feat,
        ),
    )(features, weight, bias.reshape(1, feat), cotangent, tile_values, tile_rows, tile_cols, tile_count)
    hbm = pl.BlockSpec(memory_space=pltpu.HBM)
    results = (act, gf, gw, gb)
    act, gf, gw, gb = pl.pallas_call(
        hand_over,
        out_shape=tuple(jax.ShapeDtypeStruct(a.shape, a.dtype) for a in results),
        in_specs=[hbm] * 4,
        out_specs=(hbm,) * 4,
        scratch_shapes=[pltpu.VMEM(a.shape, a.dtype) for a in results] + [pltpu.SemaphoreType.DMA((2, 4))],
        compiler_params=pltpu.CompilerParams(vmem_limit_bytes=64 * 1024 * 1024),
    )(*results)
    return act, gf, gw, gb.reshape(feat)


def solution(mesh):
    in_specs = (
        P(("row", "rep"), None),
        P(),
        P(),
        P(("row", "rep"), None),
        P("row", "rep", None, None, None),
        P("row", "rep", None),
        P("row", "rep", None),
        P("row", "rep"),
    )
    out_specs = (P(("row", "rep"), None), P(("row", "rep"), None), P(), P())
    return jax.shard_map(
        on_device, mesh=mesh, in_specs=in_specs, out_specs=out_specs, check_vma=False
    )
```

```python
import functools

import jax
import jax.numpy as jnp
from jax import lax
from jax.experimental import pallas as pl
from jax.experimental.pallas import tpu as pltpu
from jax.sharding import PartitionSpec as P

MESH = pl.DeviceIdType.MESH
F32 = jnp.float32
BF16 = jnp.bfloat16
NZ, NX, NY = 8, 4, 4
AG_SCHEMES = (
    ({0: ((3, 2), (4, -2), (1, 1), (2, -1)), 3: ((5, 1),), 4: ((6, -1),)}, (3, 4), 7, 2),
    ({0: ((3, 2), (1, 1), (2, -1))}, (), 0, 0),
    ({0: ((1, 1), (2, -1))}, (1, 2), 3, 1),
    ({0: ((3, 2), (4, -2), (1, 1), (2, -1)), 3: ((5, 1),), 4: ((6, -1),)}, (3, 4), 7, 2),
)
RS_SCHEMES = (
    ({0: ((3, 2), (4, -2), (1, 1), (2, -1)), 3: ((5, 1),), 4: ((6, -1),)}, (3, 4), 7, 2),
    ({0: ((3, 2), (1, 1), (2, -1))}, (), 0, 0),
    ({0: ((1, 1), (2, -1))}, (1, 2), 3, 1),
    ({0: ((3, 2), (4, -2), (1, 1), (2, -1)), 3: ((5, 1),), 4: ((6, -1),)}, (3, 4), 7, 2),
)
Z_REACH, X_REACH = ((1, 2), (1, 2))
AG_PARTS = ((1, 0, 96), (2, 96, 128))
RS_PARTS = ((1, 0, 96), (2, 96, 128))
AG_ORDER = (
    (0,0,0,0), (0,0,0,1), (1,0,0), (0,0,3,0), (0,3,0,0), (0,4,0,0), (0,0,1,0), (0,0,2,0), (0,1,0,0), (0,0,3,1),
    (0,2,0,0), (1,0,3), (0,0,2,1), (0,0,1,1), (1,0,2), (1,0,1), (0,3,0,1), (0,4,0,1), (1,3,0), (1,4,0), (0,1,0,1),
    (0,2,0,1), (1,1,0), (1,2,0), (2,(0,0),(0,3)), (0,3,1,0), (0,3,2,0), (2,(0,2),(0,1)), (0,5,0,0), (2,(3,0),(4,0)),
    (0,4,1,0), (0,4,2,0), (2,(1,0),(2,0)), (0,7,0,0), (0,1,1,0), (0,1,2,0), (0,3,3,1), (0,6,0,0), (0,1,3,1),
    (0,2,1,0), (0,2,2,0), (0,3,3,0), (1,3,3), (0,4,3,1), (0,3,2,1), (0,2,3,1), (1,3,2), (0,1,2,1), (1,1,2), (0,5,1,0),
    (0,5,2,0), (0,4,2,1), (1,4,2), (0,4,3,0), (1,4,3), (2,(3,3),(3,2)), (0,3,1,1), (0,2,2,1), (1,3,1), (1,2,2),
    (0,1,1,1), (1,1,1), (0,5,0,1), (1,5,0), (0,7,1,0), (0,7,2,0), (2,(1,2),(4,2)), (0,4,1,1), (1,4,1), (0,1,3,0),
    (0,2,1,1), (1,1,3), (1,2,1), (2,(4,3),(3,1)), (2,(2,2),(1,1)), (0,7,0,1), (1,7,0), (0,6,1,0), (0,6,2,0),
    (0,5,3,1), (0,6,0,1), (1,6,0), (2,(5,0),(4,1)), (0,2,3,0), (1,2,3), (0,7,3,1), (2,(1,3),(2,1)), (0,5,3,0),
    (1,5,3), (0,5,2,1), (0,6,3,1), (1,5,2), (0,7,3,0), (1,7,3), (2,(7,0),(6,0)), (0,7,2,1), (1,7,2), (2,(2,3),(5,3)),
    (0,6,3,0), (0,5,1,1), (0,6,2,1), (1,6,3), (1,5,1), (1,6,2), (2,(5,2),(7,3)), (0,7,1,1), (1,7,1), (0,6,1,1),
    (1,6,1), (2,(7,2),(6,3)), (2,(5,1),(6,2)), (2,(7,1),(6,1)),
)
RS_ORDER = (
    (2,(7,3),(5,3)), (2,(6,3),(7,1)), (2,(7,2),(5,1)), (2,(6,1),(6,2)), (2,(5,2),(4,3)), (2,(3,3),(1,3)), (0,7,3,0),
    (0,7,3,1), (0,5,3,0), (0,5,3,1), (0,6,3,0), (0,6,3,1), (2,(2,3),(7,0)), (0,7,1,1), (0,7,2,1), (2,(5,0),(6,0)),
    (0,5,1,1), (2,(3,1),(4,1)), (0,6,1,1), (0,6,2,1), (2,(4,2),(3,2)), (0,5,2,1), (2,(2,1),(1,1)), (0,4,3,0),
    (0,3,3,0), (2,(2,2),(1,2)), (0,1,3,0), (0,7,1,0), (0,7,2,0), (0,2,3,0), (0,7,0,1), (0,1,3,1), (0,5,1,0),
    (0,5,2,0), (0,3,3,1), (0,4,3,1), (0,2,3,1), (0,6,1,0), (0,6,2,0), (0,5,0,1), (0,6,0,1), (2,(4,0),(3,0)),
    (2,(0,3),(1,0)), (0,2,1,1), (0,4,1,0), (0,4,2,0), (0,1,1,1), (2,(2,0),(0,1)), (0,2,2,1), (0,3,1,0), (0,3,2,0),
    (0,1,2,1), (0,3,1,1), (0,4,1,1), (0,1,1,0), (0,4,2,1), (0,3,2,1), (0,1,2,0), (0,0,3,0), (0,1,0,1),
    (2,(0,2),(0,0)), (0,2,0,1), (0,7,0,0), (0,0,1,0), (0,2,1,0), (0,2,2,0), (0,0,2,0), (0,0,3,1), (0,5,0,0),
    (0,4,0,1), (0,3,0,1), (0,6,0,0), (0,0,1,1), (0,0,2,1), (0,1,0,0), (0,3,0,0), (0,4,0,0), (0,2,0,0), (0,0,0,1),
    (0,0,0,0),
)
G_AT = (40, 72, 77, 79)


def moves(schemes, kind, zi, xi):
    z_column, x_row, x_first, z_second = schemes
    if kind == 1:
        if xi == 0:
            yield "z", zi, z_column
        yield "x", xi, (x_first if zi else x_row)
    else:
        if zi == 0:
            yield "x", xi, x_row
        yield "z", zi, (z_second if xi else z_column)


def children(schemes, kind, zi, xi):
    found = []
    for axis, at, (steps, pair, last, hops) in moves(schemes, kind, zi, xi):
        for to, h in steps.get(at, ()):
            found.append((axis, (to, xi) if axis == "z" else (zi, to), h, None))
        if at in pair:
            found.append((axis, (last, xi) if axis == "z" else (zi, last), hops, pair.index(at)))
    return found


def body(
    tile, slots, scale,
    features_hbm, weight_hbm, bias_hbm, cotangent_hbm, values_hbm, rows_hbm, cols_hbm, count_hbm,
    act_out, gf_out, gw_out, gb_out,
    features, weight, bias, cotangent, rows, cols, count,
    values, inverse_v, inverse, gathered, acc, ysend, yrecv, dt,
    own32, own, sibsend, sibrecv, landed, back_t,
    g1s, g1r, g2s, g2r, g4r, g5, g7,
    send_sem, recv_sem, local_sem,
):
    r = lax.axis_index("row")
    y = lax.axis_index("rep")
    z = r // (2 * NX)
    x = (r // 2) % NX
    k = r % 2
    node_rows, feat = features_hbm.shape
    half = feat // 2

    def at(zz, xx, kk, yy):
        return ((zz * NX + xx) * 2 + kk, yy)

    def z_off(d):
        return at((z + d + NZ) % NZ, x, k, y)

    def x_off(d):
        return at(z, (x + d + NX) % NX, k, y)

    def y_off(d):
        return at(z, x, k, (y + d + NY) % NY)

    def toward(axis, hops, pair):
        d = hops if pair is None else hops * (1 - 2 * k)
        return z_off(d) if axis == "z" else x_off(d)

    sibling = at(z, x, 1 - k, y)
    names = {}
    groups = {}

    def copy(name, group, src, dst, device):
        i = names.setdefault(name, len(names))
        j = groups.setdefault(group, len(groups))
        return pltpu.make_async_remote_copy(
            src_ref=src, dst_ref=dst, send_sem=send_sem.at[j], recv_sem=recv_sem.at[i],
            device_id=device, device_id_type=MESH,
        )

    def send(name, group, src, dst, device):
        copy(name, group, src, dst, device).start()

    def arrived(name, dst):
        copy(name, "ag", dst, dst, sibling).wait_recv()

    def sent(group, src):
        copy("y", group, src, src, sibling).wait_send()

    loads = [
        pltpu.make_async_copy(src, dst, local_sem.at[n])
        for n, (src, dst) in enumerate((
            (features_hbm, features), (rows_hbm, rows), (cols_hbm, cols), (count_hbm, count),
            (weight_hbm, weight), (bias_hbm, bias), (cotangent_hbm, cotangent),
            (values_hbm.at[0, 0], values.at[pl.ds(0, slots)]),
        ))
    ]
    for load in loads:
        load.start()
    barrier = pltpu.get_barrier_semaphore()
    peers = (
        [z_off(s * d) for d in Z_REACH for s in (1, -1)]
        + [x_off(s * d) for d in X_REACH for s in (1, -1)]
        + [y_off(d) for d in range(1, NY)]
        + [sibling]
    )
    for p in peers:
        pl.semaphore_signal(barrier, inc=1, device_id=p, device_id_type=MESH)
    loads[0].wait()
    pl.semaphore_wait(barrier, len(peers))

    seen = set()

    def ag_piece(zi, xi, p):
        kind, r0, r1 = AG_PARTS[p]
        part = pl.ds(r0, r1 - r0)
        if (zi, xi) == (0, 0):
            source = features.at[part]
        else:
            source = gathered.at[zi, xi, 0, part]
            arrived(("ag", zi, xi, p), source)
        for axis, (zd, xd), hops, pair in children(AG_SCHEMES, kind, zi, xi):
            origin = source
            if pair is not None:
                if (zd, xd, p) not in seen:
                    seen.add((zd, xd, p))
                    continue
                if axis == "z":
                    origin = gathered.at[zi - pair + k, xi, 0, part]
                else:
                    origin = gathered.at[zi, xi - pair + k, 0, part]
            send(("ag", zd, xd, p), "ag", origin, gathered.at[zd, xd, 0, part], toward(axis, hops, pair))

    batch_of = {c: n for n, (what, *where) in enumerate(AG_ORDER) if what == 2 for c in where}

    def ag_share(zi, xi):
        source = features if (zi, xi) == (0, 0) else gathered.at[zi, xi, 0]
        send(("share", batch_of[zi, xi]), "ag", source, gathered.at[zi, xi, 1], sibling)

    def offset_of(slot):
        return (slot + 1) // 2 * (2 * (slot % 2) - 1)

    def tile_of(tr, tc):
        p = tr * (NZ * NX * 2) + tc
        return values[inverse[p // 128, p % 128]]

    def tile_pair(tr, tc_own):
        return jnp.concatenate([tile_of(tr, tc_own), tile_of(tr, tc_own + 1 - 2 * k)], axis=1)

    def col_of(zi, xi, sign):
        zz = (z + sign * offset_of(zi) + NZ) % NZ
        xx = (x + sign * offset_of(xi) + NX) % NX
        return (zz * NX + xx) * 2 + k

    def last_forward(chunks):
        arrived(("share", batch_of[chunks[0]]), gathered.at[pl.ds(0, len(chunks)), 0, 1])
        rhs = jnp.concatenate([gathered[zi, xi].reshape(2 * node_rows, feat) for zi, xi in chunks], axis=0)
        for j in (2, 1, 3, 0):
            lhs = jnp.concatenate([tile_pair((y + j) % NY, col_of(zi, xi, -1)) for zi, xi in chunks], axis=1)
            total = acc[pl.ds(j * node_rows, node_rows)] + jnp.dot(lhs, rhs, preferred_element_type=F32)
            if j == 0:
                return total
            ysend[j] = total.astype(BF16)
            send("y", "yd", ysend.at[j], yrecv.at[j], y_off(j))

    def forward(chunks):
        arrived(("share", batch_of[chunks[0]]), gathered.at[pl.ds(0, len(chunks)), 0, 1])
        lhs = jnp.concatenate([
            jnp.concatenate([tile_pair((y + j) % NY, col_of(zi, xi, -1)) for zi, xi in chunks], axis=1)
            for j in range(NY)
        ], axis=0)
        rhs = jnp.concatenate([gathered[zi, xi].reshape(2 * node_rows, feat) for zi, xi in chunks], axis=0)
        term = jnp.dot(lhs, rhs, preferred_element_type=F32)
        if (0, 0) in chunks:
            acc[...] = term
        else:
            acc[...] += term

    todo = list(AG_ORDER)
    while todo[0][:3] == (0, 0, 0):
        ag_piece(*todo.pop(0)[1:])
    gathered[0, 0, 0] = features[...]

    for load in loads[1:4]:
        load.wait()
    key = jnp.where(
        lax.broadcasted_iota(jnp.int32, (1, slots), 1) < count[...],
        rows[0] * (NZ * NX * 2) + cols[0], -1,
    )
    best = [jnp.full((1, 128), slots, jnp.int32) for _ in range(2)]
    for k0 in range(0, slots, 128):
        n = min(128, slots - k0)
        part = key[:, k0:k0 + n]
        if n < 128:
            part = jnp.concatenate([part, jnp.full((1, 128 - n), -1, jnp.int32)], axis=1)
        column = jnp.broadcast_to(part, (128, 128)).T
        slot = lax.broadcasted_iota(jnp.int32, (128, 128), 0) + k0
        for h in range(2):
            place = lax.broadcasted_iota(jnp.int32, (128, 128), 1) + h * 128
            hit = jnp.where(column == place, slot, slots)
            best[h] = jnp.minimum(best[h], jnp.min(hit, axis=0, keepdims=True))
    inverse_v[...] = jnp.concatenate(best + [jnp.full((6, 128), slots, jnp.int32)], axis=0)
    to_smem = pltpu.make_async_copy(inverse_v, inverse, local_sem.at[len(loads)])
    to_smem.start()
    values[slots] = jnp.zeros((tile, tile), BF16)

    ready = False
    final = todo.pop()
    for what, *where in todo:
        if what == 0:
            ag_piece(*where)
        elif what == 1:
            ag_share(*where)
        else:
            if not ready:
                to_smem.wait()
                for load in loads[4:]:
                    load.wait()
                ready = True
            forward(where)

    agg = last_forward(final[1:])
    arrived("y", yrecv.at[pl.ds(1, 3)])
    for j in (1, 3, 2):
        agg = agg + yrecv[j].astype(F32)
    agg_hi = agg.astype(BF16)
    agg_lo = (agg - agg_hi.astype(F32)).astype(BF16)
    halves = []
    for h in range(2):
        f = pl.ds(h * half, half)
        pre = (
            jnp.dot(agg_hi, weight[:, f], preferred_element_type=F32)
            + jnp.dot(agg_lo, weight[:, f], preferred_element_type=F32)
            + bias[:, f]
        )
        sig = jax.nn.sigmoid(pre)
        dpre = (cotangent[:, f].astype(F32) * sig * (1.0 + pre * (1.0 - sig))).astype(BF16)
        dt[0, f] = dpre.astype(F32).T.astype(BF16)
        for j in (2, 1, 3):
            send(("d", h), "yd", dt.at[0, f], dt.at[j, f], y_off(j))
        act_out[:, f] = (pre * sig).astype(BF16)
        halves.append(dpre)
    dpre = jnp.concatenate(halves, axis=1)

    aggt_hi = agg_hi.astype(F32).T.astype(BF16)
    aggt_lo = agg_lo.astype(F32).T.astype(BF16)
    bias_row = jnp.sum(dpre.astype(F32), axis=0, keepdims=True)
    bias_rows = jnp.concatenate([bias_row, jnp.zeros((7, feat), F32)], axis=0)
    gw = jnp.dot(aggt_hi, dpre, preferred_element_type=F32) + jnp.dot(
        aggt_lo, dpre, preferred_element_type=F32
    )
    for h in range(2):
        g1s[h, pl.ds(0, half)] = gw[h * half:(h + 1) * half]
        g1s[h, pl.ds(half, 8)] = bias_rows
    send("g1", "g1", g1s.at[1 - k], g1r, sibling)

    q = y * NX + x
    square = [(dy, dx) for dy in (2, 1, 3, 0) for dx in (2, 1, 3, 0) if (dy, dx) != (0, 0)]

    def in_square(dy, dx):
        yy, xx = (y + dy) % NY, (x + dx) % NX
        return yy * NX + xx, at(z, xx, k, yy)

    def g_step(n):
        if n == 0:
            arrived("g1", g1r)
            total = g1s[k] + g1r[...]
            for c in range(NY * NX):
                g2s[c, pl.ds(0, 8)] = total[c * 8:(c + 1) * 8]
                g2s[c, pl.ds(8, 8)] = total[half:half + 8]
            for dy, dx in square:
                c, device = in_square(dy, dx)
                n_rows = pl.ds(0, 16 if dy == 0 else 8)
                send("g2", "g2", g2s.at[c, n_rows], g2r.at[q, n_rows], device)
            g2r[q] = g2s[q]
        elif n == 1:
            arrived("g2", g2r.at[pl.ds(0, 9)])
            total = g2r[0, pl.ds(0, 8)]
            for c in range(1, NY * NX):
                total = total + g2r[c, pl.ds(0, 8)]
            g4r[z, pl.ds(0, 8)] = total
            total = g2r[y * NX, pl.ds(8, 8)]
            for c in range(1, NX):
                total = total + g2r[y * NX + c, pl.ds(8, 8)]
            g4r[z, pl.ds(8, 8)] = total
            for j in (4, 3, 5, 2, 6, 1, 7):
                send("g4", "g4", g4r.at[z], g4r.at[z], z_off(j))
        elif n == 2:
            arrived("g4", g4r.at[pl.ds(0, NZ - 1)])
            total = g4r[0]
            for j in range(1, NZ):
                total = total + g4r[j]
            g5[q] = total * scale
            for dy, dx in square:
                n_rows = pl.ds(0, 16 if dx == 0 else 8)
                send("g5", "g5", g5.at[q, n_rows], g5.at[q, n_rows], in_square(dy, dx)[1])
        elif n == 3:
            arrived("g5", g5.at[pl.ds(0, 9)])
            g7[k] = g5[:, pl.ds(0, 8)].reshape(half, feat)
            total = g5[x, pl.ds(8, 8)]
            for c in range(1, NY):
                total = total + g5[c * NX + x, pl.ds(8, 8)]
            gb_out[...] = total[0:1]
            send("g7", "g7", g7.at[k], g7.at[k], sibling)
        elif n == 4:
            arrived("g7", g7.at[1 - k])
            gw_out[...] = g7[...].reshape(feat, feat)

    g_step(0)
    sent("ag", values.at[pl.ds(0, 2 * (2 * NZ * NX - 1))])

    for h in range(2):
        arrived(("d", h), dt.at[pl.ds(1, NY - 1), pl.ds(h * half, half)])

    back_batch = {c: n for n, (what, *where) in enumerate(RS_ORDER) if what == 2 for c in where}
    back_size = {n: len(where) for n, (what, *where) in enumerate(RS_ORDER) if what == 2}

    def backward(chunks):
        lhs = jnp.concatenate([dt[j] for j in range(NY)], axis=1)
        for zi, xi in chunks:
            tc = col_of(zi, xi, 1)
            rhs = jnp.concatenate([tile_pair((y - j + NY) % NY, tc) for j in range(NY)], axis=0)
            both = jnp.dot(lhs, rhs, preferred_element_type=F32)
            own32[zi, xi] = both[:, :tile]
            sibsend[zi, xi] = both[:, tile:].astype(BF16)
        for zi, xi in chunks:
            send(("rss", back_batch[zi, xi]), "rs", sibsend.at[zi, xi], sibrecv.at[zi, xi], sibling)

    parent = {}
    for p, (kind, _, _) in enumerate(RS_PARTS):
        for zi in range(NZ):
            for xi in range(NX):
                for axis, (zd, xd), hops, pair in children(RS_SCHEMES, kind, zi, xi):
                    parent[zd, xd, p] = (axis, hops, pair)

    waited = set()

    def once(name, dst):
        if name not in waited:
            waited.add(name)
            arrived(name, dst)

    def rs_piece(zi, xi, p):
        kind, r0, r1 = RS_PARTS[p]
        f = pl.ds(2 * r0, 2 * (r1 - r0))
        n = back_batch[zi, xi]
        once(("rss", n), sibrecv.at[pl.ds(0, back_size[n]), 0])
        below = children(RS_SCHEMES, kind, zi, xi)
        for _, (zd, xd), _, _ in below:
            once(("rs", zd, xd, p), landed.at[zd, xd, f])
        total = own32[zi, xi, f] + sibrecv[zi, xi, f].astype(F32)
        for _, (zd, xd), _, pair in below:
            term = landed[zd, xd, f].astype(F32)
            total = total + (term if pair is None else jnp.where(k == pair, term, 0.0))
        if (zi, xi) == (0, 0):
            back_t[f] = total
            return
        own[zi, xi, f] = total.astype(BF16)
        axis, hops, pair = parent[zi, xi, p]
        send(("rs", zi, xi, p), "rs", own.at[zi, xi, f], landed.at[zi, xi, f], toward(axis, hops, pair))

    steps = {at: n + 1 for n, at in enumerate(G_AT)}
    for i, (what, *where) in enumerate(RS_ORDER):
        if what == 0:
            rs_piece(*where)
        else:
            backward(where)
        if i in steps:
            g_step(steps[i])

    gf_out[...] = lax.dot_general(
        back_t[...].T.astype(BF16), weight[...], (((1,), (1,)), ((), ())), preferred_element_type=F32
    ).astype(BF16)
    sent("yd", values.at[pl.ds(0, 4 * (NY - 1))])
    sent("rs", values.at[pl.ds(0, 2 * (2 * NZ * NX - 1))])
    sent("g1", g1r)
    sent("g2", g2r.at[pl.ds(0, 9)])
    sent("g4", g4r.at[pl.ds(0, NZ - 1)])
    sent("g5", g5.at[pl.ds(0, 9)])
    sent("g7", g7.at[0])


COPIES = 164
GROUPS = 8


def hand_over(*refs):
    count = 4
    ins, outs, held, sems = refs[:count], refs[count:2 * count], refs[2 * count:3 * count], refs[-1]
    first = [pltpu.make_async_copy(ins[n], held[n], sems.at[0, n]) for n in range(count)]
    second = [pltpu.make_async_copy(held[n], outs[n], sems.at[1, n]) for n in range(count)]
    for c in first:
        c.start()
    for c, d in zip(first, second):
        c.wait()
        d.start()
    for d in second:
        d.wait()


def on_device(features, weight, bias, cotangent, tile_values, tile_rows, tile_cols, tile_count):
    node_rows, feat = features.shape
    slots, tile = tile_values.shape[2], tile_values.shape[-1]
    half = feat // 2
    blocks = NZ * NX * 2
    scale = float((node_rows * blocks * NY) ** -0.5)
    vmem = pl.BlockSpec(memory_space=pltpu.VMEM)
    act, gf, gw, gb = pl.pallas_call(
        functools.partial(body, tile, slots, scale),
        out_shape=(
            jax.ShapeDtypeStruct((node_rows, feat), BF16),
            jax.ShapeDtypeStruct((node_rows, feat), BF16),
            jax.ShapeDtypeStruct((feat, feat), F32),
            jax.ShapeDtypeStruct((1, feat), F32),
        ),
        in_specs=[pl.BlockSpec(memory_space=pltpu.HBM)] * 8,
        out_specs=(vmem,) * 4,
        scratch_shapes=[
            pltpu.VMEM((node_rows, feat), BF16),
            pltpu.VMEM((feat, feat), BF16),
            pltpu.VMEM((1, feat), F32),
            pltpu.VMEM((node_rows, feat), BF16),
            pltpu.VMEM((1, 1, slots), jnp.int32),
            pltpu.VMEM((1, 1, slots), jnp.int32),
            pltpu.VMEM((1, 1), jnp.int32),
            pltpu.VMEM((slots + 1, tile, tile), BF16),
            pltpu.VMEM((8, 128), jnp.int32),
            pltpu.SMEM((8, 128), jnp.int32),
            pltpu.VMEM((NZ, NX, 2, node_rows, feat), BF16),
            pltpu.VMEM((NY * node_rows, feat), F32),
            pltpu.VMEM((NY, node_rows, feat), BF16),
            pltpu.VMEM((NY, node_rows, feat), BF16),
            pltpu.VMEM((NY, feat, node_rows), BF16),
            pltpu.VMEM((NZ, NX, feat, tile), F32),
            pltpu.VMEM((NZ, NX, feat, tile), BF16),
            pltpu.VMEM((NZ, NX, feat, tile), BF16),
            pltpu.VMEM((NZ, NX, feat, tile), BF16),
            pltpu.VMEM((NZ, NX, feat, tile), BF16),
            pltpu.VMEM((feat, tile), F32),
            pltpu.VMEM((2, half + 8, feat), F32),
            pltpu.VMEM((half + 8, feat), F32),
            pltpu.VMEM((NY * NX, 16, feat), F32),
            pltpu.VMEM((NY * NX, 16, feat), F32),
            pltpu.VMEM((NZ, 16, feat), F32),
            pltpu.VMEM((NY * NX, 16, feat), F32),
            pltpu.VMEM((2, half, feat), F32),
            pltpu.SemaphoreType.DMA((GROUPS,)),
            pltpu.SemaphoreType.DMA((COPIES,)),
            pltpu.SemaphoreType.DMA((9,)),
        ],
        compiler_params=pltpu.CompilerParams(
            collective_id=0, has_side_effects=True, vmem_limit_bytes=64 * 1024 * 1024
        ),
        cost_estimate=pl.CostEstimate(
            flops=4 * NY * node_rows * blocks * node_rows * feat,
            bytes_accessed=slots * tile * tile * 2,
            transcendentals=node_rows * feat,
        ),
    )(features, weight, bias.reshape(1, feat), cotangent, tile_values, tile_rows, tile_cols, tile_count)
    hbm = pl.BlockSpec(memory_space=pltpu.HBM)
    results = (act, gf, gw, gb)
    act, gf, gw, gb = pl.pallas_call(
        hand_over,
        out_shape=tuple(jax.ShapeDtypeStruct(a.shape, a.dtype) for a in results),
        in_specs=[hbm] * 4,
        out_specs=(hbm,) * 4,
        scratch_shapes=[pltpu.VMEM(a.shape, a.dtype) for a in results] + [pltpu.SemaphoreType.DMA((2, 4))],
        compiler_params=pltpu.CompilerParams(vmem_limit_bytes=64 * 1024 * 1024),
    )(*results)
    return act, gf, gw, gb.reshape(feat)


def solution(mesh):
    in_specs = (
        P(("row", "rep"), None),
        P(),
        P(),
        P(("row", "rep"), None),
        P("row", "rep", None, None, None),
        P("row", "rep", None),
        P("row", "rep", None),
        P("row", "rep"),
    )
    out_specs = (P(("row", "rep"), None), P(("row", "rep"), None), P(), P())
    return jax.shard_map(
        on_device, mesh=mesh, in_specs=in_specs, out_specs=out_specs, check_vma=False
    )
```
